32 devices in a mesh: space: 16 (over z, y, x), batch: 2 (over core).
Axes of the slice: x: 2, y: 2, z: 4, core: 2. Of those that a mesh axis runs over, the one named last changes fastest.
Arguments:
- features: bfloat16 [2, 8192, 128], P('batch', 'space'), may hold values from -6 to 6
- weights: bfloat16 [27, 128, 128], replicated, may hold values from -0.109375 to 0.109375
- kernel_map: int32 [2, 27, 8192], P('batch', None, 'space'), may hold values from 0 to 768, as said below
- send_rows: int32 [2, 2, 2048], P('batch', None, 'space'), may hold values from 0 to 511, as said below
- counts: int32 [2, 16], P('batch', 'space'), may hold values from 64 to 512, as said below
- cotangent: bfloat16 [2, 8192, 128], P('batch', 'space'), may hold values from -6 to 6
Outputs:
- output: bfloat16 [2, 8192, 128], P('batch', 'space')
- grad_features: bfloat16 [2, 8192, 128], P('batch', 'space')
- grad_weights: float32 [27, 128, 128], replicated
The draws below stay inside these ranges and needn't reach their ends.
Inputs may be any that keep to these rules, and one draw needn't show every extreme that they name: `kernel_map`: values below 512 are active slots of the same block (below its count); 512 to 639 are rows received from the lower block, the next 128 rows from the upper block, 768 is the zero row. The first block never reads the lower rows, the last never the upper ones. The middle offset reads each active slot itself; inactive slots read only the zero row. `send_rows`: every entry is an active slot of the sending block. `counts`: each scene tile has a block with all 512 slots active and a block with exactly 64; every block has at least 64.
All inputs are finite; a program needn't handle non-finite values.
Results may differ from the reference program's by a relative error of at most 0.001.
Values may be sent and summed in bfloat16 or wider, within the bound.
A program may use at most 64 MiB of HBM per device.

```python
import jax
import jax.numpy as jnp
from jax import lax

C = 128
KV = 27
VOX = 512
HALO = 128
ROWS = 8192
SCENES = 2
N_SPACE = 16


def geometry(key):
    blocks = ROWS // VOX
    counts = jax.random.randint(jax.random.fold_in(key, 11), (SCENES, blocks), VOX // 8, VOX + 1)
    full_block = jax.random.randint(jax.random.fold_in(key, 12), (SCENES, 1), 0, blocks)
    small_block = (full_block + 1) % blocks
    block_line = jnp.arange(blocks)[None, :]
    counts = jnp.where(block_line == small_block, VOX // 8, counts)
    counts = jnp.where(block_line == full_block, VOX, counts).astype(jnp.int32)
    drawn_rows = jax.random.randint(jax.random.fold_in(key, 13), (SCENES, 2, blocks, HALO), 0, VOX)
    picked = drawn_rows % counts[:, None, :, None]
    entry_index = jnp.arange(HALO)[None, None, None, :]
    picked = jnp.where(entry_index == 0, counts[:, None, :, None] - 1, picked)
    picked = jnp.where(entry_index == 1, 0, picked)
    send_lists = picked.reshape(SCENES, 2, blocks * HALO).astype(jnp.int32)
    shape = (SCENES, KV, blocks, VOX)
    kind_draw = jax.random.randint(jax.random.fold_in(key, 14), shape, 0, 100)
    local_rows = jax.random.randint(jax.random.fold_in(key, 15), shape, 0, VOX) % counts[:, None, :, None]
    side_pick = jax.random.randint(jax.random.fold_in(key, 16), shape, 0, 2)
    block_index = jnp.arange(blocks)[None, None, :, None]
    side_pick = jnp.where(block_index == 0, 1, jnp.where(block_index == blocks - 1, 0, side_pick))
    halo_slot = VOX + side_pick * HALO + jax.random.randint(jax.random.fold_in(key, 17), shape, 0, HALO)
    sentinel = VOX + 2 * HALO
    offset_map = jnp.where(kind_draw < 30, local_rows, jnp.where(kind_draw < 40, halo_slot, sentinel))
    row_index = jnp.arange(VOX)[None, None, None, :]
    is_centre = jnp.arange(KV)[None, :, None, None] == KV // 2
    offset_map = jnp.where(is_centre, row_index, offset_map)
    offset_map = jnp.where(row_index < counts[:, None, :, None], offset_map, sentinel)
    return (counts, send_lists, offset_map.reshape(SCENES, KV, blocks * VOX).astype(jnp.int32))


def draw_kernel_map(key, part):
    return geometry(key)[2]


def draw_send_rows(key, part):
    return geometry(key)[1]


def draw_counts(key, part):
    return geometry(key)[0]


def block_scale(rng, shape, shards, low, top_value):
    gain = 1.0
    for dim, shards_of in shards:
        heights = jax.random.uniform(jax.random.fold_in(jax.random.fold_in(rng, 6), dim), (shards_of,), jnp.float32, low / len(shards), top_value / len(shards))
        gain = gain * jnp.repeat(jnp.exp(heights), shape[dim] // shards_of).reshape((-1,) + (1,) * (len(shape) - 1 - dim))
    return gain


def noise(rng, dims, spread, bound, split=(), held_as=jnp.bfloat16):
    values = spread * jax.random.normal(rng, dims, jnp.float32)
    if split:
        values = values * block_scale(rng, dims, split, -0.22, 0.18)
    return jnp.clip(values, -bound, bound).astype(held_as)


def setup_inputs(seed: int = 0) -> dict:
    splits = jax.random.split(jax.random.key(seed), 7)
    return {
        "features": noise(splits[0], (SCENES, ROWS, C), 1.0, 6.0, ((0, 2), (1, 16))),
        "weights": noise(splits[1], (KV, C, C), (KV * C) ** -0.5, 0.109375),
        "kernel_map": draw_kernel_map(jax.random.fold_in(splits[6], 71), 0),
        "send_rows": draw_send_rows(jax.random.fold_in(splits[6], 71), 0),
        "counts": draw_counts(jax.random.fold_in(splits[6], 71), 0),
        "cotangent": noise(splits[5], (SCENES, ROWS, C), 1.0, 6.0, ((0, 2), (1, 16))),
    }


def pick_rows(table, indices):
    return table[indices]


def add_back(local_grads, send_lists, for_upper, for_lower):
    return local_grads.at[send_lists[1]].add(for_upper).at[send_lists[0]].add(for_lower)


def reference(features, weights, kernel_map, send_rows, counts, cotangent):
    block_count = SCENES * N_SPACE
    ext_length = VOX + 2 * HALO + 1
    active = jnp.arange(VOX, dtype=jnp.int32)[None, None, :] < counts[:, :, None]
    blocks = features.reshape(SCENES, N_SPACE, VOX, C)
    live = jnp.where(active[..., None], blocks, jnp.zeros((), jnp.bfloat16))
    zero_row = jnp.zeros((SCENES, N_SPACE, 1, C), jnp.bfloat16)
    padded = jnp.concatenate([live, zero_row], 2)
    send_lists = send_rows.reshape(SCENES, 2, N_SPACE, HALO).transpose(0, 2, 1, 3)
    outgoing = jax.vmap(jax.vmap(pick_rows))(padded, send_lists)
    zeros_halo = jnp.zeros((SCENES, 1, HALO, C), jnp.bfloat16)
    lower_in = jnp.concatenate([zeros_halo, outgoing[:, :-1, 1]], 1)
    upper_in = jnp.concatenate([outgoing[:, 1:, 0], zeros_halo], 1)
    extended = jnp.concatenate([live, lower_in, upper_in, zero_row], 2).reshape(block_count, ext_length, C)
    offset_maps = kernel_map.reshape(SCENES, KV, N_SPACE, VOX).transpose(0, 2, 1, 3).reshape(block_count, KV, VOX)
    alive = active.reshape(block_count, VOX, 1)
    grad_out = jnp.where(alive, cotangent.reshape(block_count, VOX, C), jnp.zeros((), jnp.bfloat16))

    def one_block(weight_total, inputs):
        table, offset_map, alive_rows, grad_rows = inputs

        def forward_step(running, pair):
            source, weight = pair
            return running + jnp.dot(table[source], weight, preferred_element_type=jnp.float32), None

        result, unused = lax.scan(forward_step, jnp.zeros((VOX, C), jnp.float32), (offset_map, weights))
        result = jnp.where(alive_rows, result, jnp.zeros((), jnp.float32)).astype(jnp.bfloat16)

        def backward_step(accum_grad, pair):
            source, weight = pair
            gathered = table[source]
            weight_part = lax.dot_general(gathered, grad_rows, (((0,), (0,)), ((), ())), preferred_element_type=jnp.float32)
            contrib = jnp.dot(grad_rows, weight.T, preferred_element_type=jnp.float32)
            return accum_grad.at[source].add(contrib), weight_part

        ext_grad, weight_parts = lax.scan(backward_step, jnp.zeros((ext_length, C), jnp.float32), (offset_map, weights))
        return weight_total + weight_parts, (result, ext_grad)

    weight_total, (results, ext_grads) = lax.scan(one_block, jnp.zeros((KV, C, C), jnp.float32), (extended, offset_maps, alive, grad_out))
    ext_grads = ext_grads.reshape(SCENES, N_SPACE, ext_length, C)
    lower_part = ext_grads[:, :, VOX:VOX + HALO]
    upper_part = ext_grads[:, :, VOX + HALO:VOX + 2 * HALO]
    zeros_grad = jnp.zeros((SCENES, 1, HALO, C), jnp.float32)
    for_upper = jnp.concatenate([lower_part[:, 1:], zeros_grad], 1)
    for_lower = jnp.concatenate([zeros_grad, upper_part[:, :-1]], 1)
    local_grads = jnp.concatenate([ext_grads[:, :, :VOX], jnp.zeros((SCENES, N_SPACE, 1, C), jnp.float32)], 2)
    local_grads = jax.vmap(jax.vmap(add_back))(local_grads, send_lists, for_upper, for_lower)
    grad_features = jnp.where(active[..., None], local_grads[:, :, :VOX], jnp.zeros((), jnp.float32)).astype(jnp.bfloat16)
    output = results.reshape(SCENES, ROWS, C)
    grad_weights = weight_total * ((SCENES * ROWS) ** -0.5)
    return output, grad_features.reshape(SCENES, ROWS, C), grad_weights
```

```python
import functools

import jax
import jax.numpy as jnp
from jax import lax
from jax.experimental import pallas as pl
from jax.experimental.pallas import tpu as pltpu
from jax.sharding import PartitionSpec as P

F32 = jnp.float32
BF16 = jnp.bfloat16
MESH = pl.DeviceIdType.MESH
GROUPS = 3
BATCH = 3
TILES = 16
ROW = 8


def dot(a, b, contract=((1,), (0,))):
    return lax.dot_general(a, b, (contract, ((), ())), preferred_element_type=F32)


def onehot_columns(row, height):
    line = lax.broadcasted_iota(jnp.int32, (height, row.shape[1]), 0)
    return jnp.where(line == row, jnp.ones((), F32), jnp.zeros((), F32)).astype(BF16)


def split_pair(x):
    high = x.astype(BF16)
    low = (x - high.astype(F32)).astype(BF16)
    return jnp.concatenate([high, low], 1)


def mesh_bits(n_space, n_batch):
    bits = [("batch", 1)] if n_batch > 1 else []
    weight = 1
    while weight < n_space:
        bits.append(("space", weight))
        weight *= 2
    weight = 2
    while weight < n_batch:
        bits.append(("batch", weight))
        weight *= 2
    return bits


def plan(n_space, n_batch):
    bits = mesh_bits(n_space, n_batch)
    halvings = min(4, len(bits))
    orders = []
    for q in range(GROUPS):
        rest = bits[1:halvings]
        turn = q % max(len(rest), 1)
        orders.append(bits[:1] + rest[turn:] + rest[:turn])
    return orders, bits[halvings:]


def kernel(
    n_space, n_batch, scale,
    feat, w, kmap, send, count, cot,
    out, gfeat, gw,
    ext, outgoing, extt, grad, gt, dw, inbox, acc, gext, back, outt,
    halo_send, halo_recv, back_send, back_recv, sum_send, sum_recv,
):
    offsets, channels = w.shape[0], w.shape[1]
    slots = feat.shape[0]
    halo = send.shape[1]
    table = slots + 2 * halo
    per_group = offsets // GROUPS
    here = {"space": lax.axis_index("space"), "batch": lax.axis_index("batch")}
    s = here["space"]
    orders, full = plan(n_space, n_batch)
    halvings = len(orders[0])

    def bit_of(bit):
        return (here[bit[0]] // bit[1]) % 2

    def partner(bit):
        return {**here, bit[0]: here[bit[0]] + bit[1] * (1 - 2 * bit_of(bit))}

    lower = {**here, "space": s - 1}
    upper = {**here, "space": s + 1}
    has_lower = s > 0
    has_upper = s < n_space - 1

    barrier = pltpu.get_barrier_semaphore()
    for bit in orders[0] + full:
        pl.semaphore_signal(barrier, inc=1, device_id=partner(bit), device_id_type=MESH)

    @pl.when(has_lower)
    def _():
        pl.semaphore_signal(barrier, inc=1, device_id=lower, device_id_type=MESH)

    @pl.when(has_upper)
    def _():
        pl.semaphore_signal(barrier, inc=1, device_id=upper, device_id_type=MESH)

    alive = lax.broadcasted_iota(jnp.int32, (slots, channels), 0) < count[0, 0]
    live = jnp.where(alive, feat[...].astype(F32), jnp.zeros((), F32)).astype(BF16)
    ext[:slots] = live
    grad[...] = jnp.where(alive, cot[...].astype(F32), jnp.zeros((), F32)).astype(BF16)
    lists = jnp.concatenate([send[0:1, :], send[1:2, :]], 1)
    outgoing[...] = dot(onehot_columns(lists, slots), live, ((0,), (0,))).astype(BF16)

    @pl.when(s == 0)
    def _():
        ext[slots : slots + halo] = jnp.zeros((halo, channels), BF16)
        back[halo:] = jnp.zeros((halo, channels), F32)

    @pl.when(s == n_space - 1)
    def _():
        ext[slots + halo :] = jnp.zeros((halo, channels), BF16)
        back[:halo] = jnp.zeros((halo, channels), F32)

    neighbours = 1 * (jnp.minimum(s, 1) + jnp.minimum(n_space - 1 - s, 1))
    pl.semaphore_wait(barrier, len(orders[0] + full) + neighbours)

    to_lower = pltpu.make_async_remote_copy(
        src_ref=outgoing.at[:halo], dst_ref=ext.at[pl.ds(slots + halo, halo)],
        send_sem=halo_send.at[0], recv_sem=halo_recv.at[0], device_id=lower, device_id_type=MESH)
    to_upper = pltpu.make_async_remote_copy(
        src_ref=outgoing.at[pl.ds(halo, halo)], dst_ref=ext.at[pl.ds(slots, halo)],
        send_sem=halo_send.at[1], recv_sem=halo_recv.at[1], device_id=upper, device_id_type=MESH)

    def start_both(down, up):
        @pl.when(has_lower)
        def _():
            down.start()

        @pl.when(has_upper)
        def _():
            up.start()

    def wait_both(down, up):
        @pl.when(has_lower)
        def _():
            down.wait_send()
            up.wait_recv()

        @pl.when(has_upper)
        def _():
            up.wait_send()
            down.wait_recv()

    start_both(to_lower, to_upper)

    steps = halvings + len(full) + halvings
    place = [0] * GROUPS
    begin = [[0] for _ in range(GROUPS)]
    flying = [None] * GROUPS

    def launch(q):
        step = place[q]
        ks = pl.ds(q * per_group, per_group)
        sem = q * steps + step
        if step < halvings:
            bit = orders[q][step]
            size = TILES >> (step + 1)
            src = dw.at[ks, pl.ds(begin[q][-1] + (1 - bit_of(bit)) * size, size)]
            dst = inbox.at[ks, pl.ds(TILES - 2 * size, size)]
        elif step < halvings + len(full):
            bit = full[step - halvings]
            size = TILES >> halvings
            src = dw.at[ks, pl.ds(begin[q][-1], size)]
            dst = inbox.at[ks, pl.ds(TILES - size + (step - halvings) * size, size)]
        else:
            level = steps - 1 - step
            bit = orders[q][level]
            size = TILES >> (level + 1)
            src = gw.at[ks, pl.ds(begin[q][level + 1], size)]
            dst = gw.at[ks, pl.ds(begin[q][level + 1], size)]
        flying[q] = pltpu.make_async_remote_copy(
            src_ref=src, dst_ref=dst, send_sem=sum_send.at[sem], recv_sem=sum_recv.at[sem],
            device_id=partner(bit), device_id_type=MESH)
        flying[q].start()

    def advance(q):
        step = place[q]
        if step >= steps:
            return
        flying[q].wait()
        ks = pl.ds(q * per_group, per_group)
        if step < halvings + len(full):
            if step < halvings:
                size = TILES >> (step + 1)
                at = begin[q][-1] + bit_of(orders[q][step]) * size
                begin[q].append(at)
                got = pl.ds(TILES - 2 * size, size)
            else:
                size = TILES >> halvings
                at = begin[q][-1]
                got = pl.ds(TILES - size + (step - halvings) * size, size)
            mine = pl.ds(at, size)
            total = dw[ks, mine] + inbox[ks, got]
            if step == halvings + len(full) - 1:
                gw[ks, mine] = total * scale
            else:
                dw[ks, mine] = total
        place[q] = step + 1
        if place[q] < steps:
            launch(q)

    def advance_all():
        for q in range(GROUPS):
            advance(q)

    acc[...] = jnp.zeros_like(acc)
    outt[...] = jnp.zeros_like(outt)
    wait_both(to_lower, to_upper)
    extt[...] = ext[...].astype(F32).T.astype(BF16)

    def weight_step(j, carry):
        for t in range(BATCH):
            k = j * BATCH + t
            picked = onehot_columns(kmap[pl.ds(k, 1), :], table)
            gathered = dot(extt[...], picked).astype(BF16)
            gt[pl.ds(pl.multiple_of(k * channels, channels), channels)] = gathered
            dw[k] = dot(gathered, grad[...]).reshape(TILES, ROW, channels)
        return carry

    def scatter_step(j, carry):
        weights = w[pl.ds(j * BATCH, BATCH)].reshape(BATCH * channels, channels)
        contrib = dot(grad[...], weights, ((1,), (1,)))
        picks, parts = [], []
        for t in range(BATCH):
            picks.append(onehot_columns(kmap[pl.ds(j * BATCH + t, 1), :], table))
            parts.append(split_pair(contrib[:, t * channels : (t + 1) * channels]))
        acc[...] += dot(jnp.concatenate(picks, 1), jnp.concatenate(parts, 0))
        return carry

    def forward_step(j, carry):
        weights = w[pl.ds(j * BATCH, BATCH)].reshape(BATCH * channels, channels)
        size = BATCH * channels
        rows = gt[pl.ds(pl.multiple_of(j * size, size), size)]
        outt[...] += dot(weights, rows, ((0,), (0,)))
        return carry

    loops = per_group // BATCH
    for q in range(GROUPS):
        lax.fori_loop(q * loops, (q + 1) * loops, weight_step, 0)
        for earlier in range(q):
            advance(earlier)
        launch(q)

    total_loops = offsets // BATCH
    for j in range(0, total_loops, 2):
        lax.fori_loop(j, min(j + 2, total_loops), scatter_step, 0)
        advance_all()

    both = acc[...]
    gext[...] = both[:, :channels] + both[:, channels:]
    back_lower = pltpu.make_async_remote_copy(
        src_ref=gext.at[pl.ds(slots, halo)], dst_ref=back.at[:halo],
        send_sem=back_send.at[0], recv_sem=back_recv.at[0], device_id=lower, device_id_type=MESH)
    back_upper = pltpu.make_async_remote_copy(
        src_ref=gext.at[pl.ds(slots + halo, halo)], dst_ref=back.at[pl.ds(halo, halo)],
        send_sem=back_send.at[1], recv_sem=back_recv.at[1], device_id=upper, device_id_type=MESH)
    start_both(back_lower, back_upper)

    lax.fori_loop(0, total_loops, forward_step, 0)
    out[...] = jnp.where(alive, outt[...].T, jnp.zeros((), F32)).astype(BF16)
    advance_all()

    wait_both(back_lower, back_upper)
    lists = jnp.concatenate([send[1:2, :], send[0:1, :]], 1)
    extra = dot(onehot_columns(lists, slots), split_pair(back[...]))
    local = gext[:slots] + extra[:, :channels] + extra[:, channels:]
    gfeat[...] = jnp.where(alive, local, jnp.zeros((), F32)).astype(BF16)

    while min(place) < steps:
        advance_all()


def per_device(n_space, n_batch, features, weights, kernel_map, send_rows, counts, cotangent):
    slots, channels = features.shape[1], features.shape[2]
    offsets = weights.shape[0]
    halo = send_rows.shape[2]
    table = slots + 2 * halo
    orders, full = plan(n_space, n_batch)
    steps = 2 * len(orders[0]) + len(full)
    vmem = pl.BlockSpec(memory_space=pltpu.VMEM)
    smem = pl.BlockSpec(memory_space=pltpu.SMEM)
    scale = float((slots * n_space * n_batch) ** -0.5)
    result, grad_features, grad_weights = pl.pallas_call(
        functools.partial(kernel, n_space, n_batch, scale),
        out_shape=(
            jax.ShapeDtypeStruct((slots, channels), BF16),
            jax.ShapeDtypeStruct((slots, channels), BF16),
            jax.ShapeDtypeStruct((offsets, TILES, ROW, channels), F32),
        ),
        in_specs=[vmem, vmem, vmem, vmem, smem, vmem],
        out_specs=(vmem, vmem, vmem),
        scratch_shapes=[
            pltpu.VMEM((table, channels), BF16),
            pltpu.VMEM((2 * halo, channels), BF16),
            pltpu.VMEM((channels, table), BF16),
            pltpu.VMEM((slots, channels), BF16),
            pltpu.VMEM((offsets * channels, slots), BF16),
            pltpu.VMEM((offsets, TILES, ROW, channels), F32),
            pltpu.VMEM((offsets, TILES + len(full), ROW, channels), F32),
            pltpu.VMEM((table, 2 * channels), F32),
            pltpu.VMEM((table, channels), F32),
            pltpu.VMEM((2 * halo, channels), F32),
            pltpu.VMEM((channels, slots), F32),
            pltpu.SemaphoreType.DMA((2,)),
            pltpu.SemaphoreType.DMA((2,)),
            pltpu.SemaphoreType.DMA((2,)),
            pltpu.SemaphoreType.DMA((2,)),
            pltpu.SemaphoreType.DMA((GROUPS * steps,)),
            pltpu.SemaphoreType.DMA((GROUPS * steps,)),
        ],
        compiler_params=pltpu.CompilerParams(
            collective_id=0, has_side_effects=True, vmem_limit_bytes=48 * 1024 * 1024
        ),
        name="sparse_conv",
    )(features[0], weights, kernel_map[0], send_rows[0], counts, cotangent[0])
    return (
        result[None],
        grad_features[None],
        grad_weights.reshape(offsets, channels, channels),
    )


def solution(mesh):
    in_specs = (
        P("batch", "space", None),
        P(),
        P("batch", None, "space"),
        P("batch", None, "space"),
        P("batch", "space"),
        P("batch", "space", None),
    )
    out_specs = (P("batch", "space", None), P("batch", "space", None), P())
    body = functools.partial(per_device, mesh.shape["space"], mesh.shape["batch"])
    return jax.shard_map(body, mesh=mesh, in_specs=in_specs, out_specs=out_specs, check_vma=False)
```

```python
import functools

import jax
import jax.numpy as jnp
from jax import lax
from jax.experimental import pallas as pl
from jax.experimental.pallas import tpu as pltpu
from jax.sharding import PartitionSpec as P

F32 = jnp.float32
BF16 = jnp.bfloat16
MESH = pl.DeviceIdType.MESH
BATCH = 3
SIZES = (4, 3, 2)
GROUPS = len(SIZES)
EARLY = 2
TILES = 16
ROW = 8


def dot(a, b, contract=((1,), (0,))):
    return lax.dot_general(a, b, (contract, ((), ())), preferred_element_type=F32)


def onehot_columns(row, height):
    line = lax.broadcasted_iota(jnp.int16, (height, row.shape[1]), 0)
    hit = line == jnp.broadcast_to(row.astype(jnp.int16), line.shape)
    return jnp.where(hit, jnp.ones((), BF16), jnp.zeros((), BF16))


def split_pair(x):
    high = x.astype(BF16)
    low = (x - high.astype(F32)).astype(BF16)
    return jnp.concatenate([high, low], 1)


def mesh_bits(n_space, n_batch):
    bits = [("batch", 1)] if n_batch > 1 else []
    weight = 1
    while weight < n_space:
        bits.append(("space", weight))
        weight *= 2
    weight = 2
    while weight < n_batch:
        bits.append(("batch", weight))
        weight *= 2
    return bits


def plan(n_space, n_batch):
    bits = mesh_bits(n_space, n_batch)
    halvings = min(4, len(bits))
    orders = []
    for q in range(GROUPS):
        rest = bits[1:halvings]
        turn = q % max(len(rest), 1)
        orders.append(bits[:1] + rest[turn:] + rest[:turn])
    return orders, bits[halvings:]


def kernel(
    n_space, n_batch, scale,
    feat_hbm, w_hbm, kmap_hbm, send_hbm, count, cot_hbm,
    out, gfeat, gw,
    feat, w, kmap, send, cot, load_sem,
    ext, outgoing, extt, grad, gt, dw, inbox, acc, gext, back, outt,
    halo_send, halo_recv, back_send, back_recv, sum_send, sum_recv,
):
    offsets, channels = w.shape[0], w.shape[1]
    slots = feat.shape[0]
    halo = send.shape[1]
    table = slots + 2 * halo
    firsts = [BATCH * sum(SIZES[:q]) for q in range(GROUPS)]
    here = {"space": lax.axis_index("space"), "batch": lax.axis_index("batch")}
    s = here["space"]
    orders, full = plan(n_space, n_batch)
    halvings = len(orders[0])

    def bit_of(bit):
        return (here[bit[0]] // bit[1]) % 2

    def partner(bit):
        return {**here, bit[0]: here[bit[0]] + bit[1] * (1 - 2 * bit_of(bit))}

    lower = {**here, "space": s - 1}
    upper = {**here, "space": s + 1}
    has_lower = s > 0
    has_upper = s < n_space - 1

    loads = {}
    pairs = dict(feat=(feat_hbm, feat), send=(send_hbm, send), cot=(cot_hbm, cot), kmap=(kmap_hbm, kmap), w=(w_hbm, w))
    for n, (name, (src, dst)) in enumerate(pairs.items()):
        loads[name] = pltpu.make_async_copy(src, dst, load_sem.at[n])
        loads[name].start()

    barrier = pltpu.get_barrier_semaphore()
    for bit in orders[0] + full:
        pl.semaphore_signal(barrier, inc=1, device_id=partner(bit), device_id_type=MESH)

    @pl.when(has_lower)
    def _():
        pl.semaphore_signal(barrier, inc=1, device_id=lower, device_id_type=MESH)

    @pl.when(has_upper)
    def _():
        pl.semaphore_signal(barrier, inc=1, device_id=upper, device_id_type=MESH)

    alive = lax.broadcasted_iota(jnp.int32, (slots, channels), 0) < count[0, 0]
    loads["feat"].wait()
    live = jnp.where(alive, feat[...].astype(F32), jnp.zeros((), F32)).astype(BF16)
    ext[:slots] = live
    loads["send"].wait()
    lists = jnp.concatenate([send[0:1, :], send[1:2, :]], 1)
    outgoing[...] = dot(onehot_columns(lists, slots), live, ((0,), (0,))).astype(BF16)

    @pl.when(s == 0)
    def _():
        ext[slots : slots + halo] = jnp.zeros((halo, channels), BF16)
        back[halo:] = jnp.zeros((halo, channels), F32)

    @pl.when(s == n_space - 1)
    def _():
        ext[slots + halo :] = jnp.zeros((halo, channels), BF16)
        back[:halo] = jnp.zeros((halo, channels), F32)

    neighbours = 1 * (jnp.minimum(s, 1) + jnp.minimum(n_space - 1 - s, 1))
    pl.semaphore_wait(barrier, len(orders[0] + full) + neighbours)

    to_lower = pltpu.make_async_remote_copy(
        src_ref=outgoing.at[:halo], dst_ref=ext.at[pl.ds(slots + halo, halo)],
        send_sem=halo_send.at[0], recv_sem=halo_recv.at[0], device_id=lower, device_id_type=MESH)
    to_upper = pltpu.make_async_remote_copy(
        src_ref=outgoing.at[pl.ds(halo, halo)], dst_ref=ext.at[pl.ds(slots, halo)],
        send_sem=halo_send.at[1], recv_sem=halo_recv.at[1], device_id=upper, device_id_type=MESH)

    def start_both(down, up):
        @pl.when(has_lower)
        def _():
            down.start()

        @pl.when(has_upper)
        def _():
            up.start()

    def wait_both(down, up):
        @pl.when(has_lower)
        def _():
            down.wait_send()
            up.wait_recv()

        @pl.when(has_upper)
        def _():
            up.wait_send()
            down.wait_recv()

    start_both(to_lower, to_upper)

    steps = halvings + len(full) + halvings
    place = [0] * GROUPS
    begin = [[0] for _ in range(GROUPS)]
    flying = [None] * GROUPS

    def launch(q):
        step = place[q]
        ks = pl.ds(firsts[q], BATCH * SIZES[q])
        sem = q * steps + step
        if step < halvings:
            bit = orders[q][step]
            size = TILES >> (step + 1)
            src = dw.at[ks, pl.ds(begin[q][-1] + (1 - bit_of(bit)) * size, size)]
            dst = inbox.at[ks, pl.ds(TILES - 2 * size, size)]
        elif step < halvings + len(full):
            bit = full[step - halvings]
            size = TILES >> halvings
            src = dw.at[ks, pl.ds(begin[q][-1], size)]
            dst = inbox.at[ks, pl.ds(TILES - size + (step - halvings) * size, size)]
        else:
            level = steps - 1 - step
            bit = orders[q][level]
            size = TILES >> (level + 1)
            src = gw.at[ks, pl.ds(begin[q][level + 1], size)]
            dst = gw.at[ks, pl.ds(begin[q][level + 1], size)]
        flying[q] = pltpu.make_async_remote_copy(
            src_ref=src, dst_ref=dst, send_sem=sum_send.at[sem], recv_sem=sum_recv.at[sem],
            device_id=partner(bit), device_id_type=MESH)
        flying[q].start()

    def advance(q):
        step = place[q]
        if step >= steps:
            return
        flying[q].wait()
        ks = pl.ds(firsts[q], BATCH * SIZES[q])
        if step < halvings + len(full):
            if step < halvings:
                size = TILES >> (step + 1)
                at = begin[q][-1] + bit_of(orders[q][step]) * size
                begin[q].append(at)
                got = pl.ds(TILES - 2 * size, size)
            else:
                size = TILES >> halvings
                at = begin[q][-1]
                got = pl.ds(TILES - size + (step - halvings) * size, size)
            mine = pl.ds(at, size)
            total = dw[ks, mine] + inbox[ks, got]
            if step == halvings + len(full) - 1:
                gw[ks, mine] = total * scale
            else:
                dw[ks, mine] = total
        place[q] = step + 1
        if place[q] < steps:
            launch(q)

    def advance_all():
        for q in range(GROUPS):
            advance(q)

    acc[...] = jnp.zeros_like(acc)
    outt[...] = jnp.zeros_like(outt)
    loads["cot"].wait()
    grad[...] = jnp.where(alive, cot[...].astype(F32), jnp.zeros((), F32)).astype(BF16)
    loads["kmap"].wait()
    loads["w"].wait()
    def scatter_step(j, carry):
        weights = w[pl.ds(j * BATCH, BATCH)].reshape(BATCH * channels, channels)
        contrib = dot(grad[...], weights, ((1,), (1,)))
        picks, parts = [], []
        for t in range(BATCH):
            picks.append(onehot_columns(kmap[j * BATCH + t], table))
            parts.append(split_pair(contrib[:, t * channels : (t + 1) * channels]))
        acc[...] += dot(jnp.concatenate(picks, 1), jnp.concatenate(parts, 0))
        return carry

    lax.fori_loop(0, EARLY, scatter_step, 0)
    wait_both(to_lower, to_upper)
    extt[...] = ext[...].astype(F32).T.astype(BF16)

    def weight_step(j, carry):
        for t in range(BATCH):
            k = j * BATCH + t
            picked = onehot_columns(kmap[k], table)
            gathered = dot(extt[...], picked).astype(BF16)
            gt[pl.ds(pl.multiple_of(k * channels, channels), channels)] = gathered
            dw[k] = dot(gathered, grad[...]).reshape(TILES, ROW, channels)
        return carry

    def forward_step(j, carry):
        weights = w[pl.ds(j * BATCH, BATCH)].reshape(BATCH * channels, channels)
        size = BATCH * channels
        rows = gt[pl.ds(pl.multiple_of(j * size, size), size)]
        outt[...] += dot(weights, rows, ((0,), (0,)))
        return carry

    total_loops = offsets // BATCH
    lax.fori_loop(0, 4, weight_step, 0)
    launch(0)
    lax.fori_loop(4, 5, weight_step, 0)
    advance(0)
    lax.fori_loop(5, 7, weight_step, 0)
    launch(1)
    lax.fori_loop(7, 8, weight_step, 0)
    advance(0)
    advance(1)
    lax.fori_loop(8, total_loops, weight_step, 0)
    launch(2)
    for j in range(EARLY, total_loops):
        lax.fori_loop(j, j + 1, scatter_step, 0)
        advance_all()

    both = acc[...]
    gext[...] = both[:, :channels] + both[:, channels:]
    back_lower = pltpu.make_async_remote_copy(
        src_ref=gext.at[pl.ds(slots, halo)], dst_ref=back.at[:halo],
        send_sem=back_send.at[0], recv_sem=back_recv.at[0], device_id=lower, device_id_type=MESH)
    back_upper = pltpu.make_async_remote_copy(
        src_ref=gext.at[pl.ds(slots + halo, halo)], dst_ref=back.at[pl.ds(halo, halo)],
        send_sem=back_send.at[1], recv_sem=back_recv.at[1], device_id=upper, device_id_type=MESH)
    start_both(back_lower, back_upper)

    lax.fori_loop(0, 5, forward_step, 0)
    advance_all()
    lax.fori_loop(5, total_loops, forward_step, 0)
    out[...] = jnp.where(alive, outt[...].T, jnp.zeros((), F32)).astype(BF16)
    advance_all()

    wait_both(back_lower, back_upper)
    lists = jnp.concatenate([send[1:2, :], send[0:1, :]], 1)
    extra = dot(onehot_columns(lists, slots), split_pair(back[...]))
    local = gext[:slots] + extra[:, :channels] + extra[:, channels:]
    gfeat[...] = jnp.where(alive, local, jnp.zeros((), F32)).astype(BF16)

    while min(place) < steps:
        advance_all()


def per_device(n_space, n_batch, features, weights, kernel_map, send_rows, counts, cotangent):
    slots, channels = features.shape[1], features.shape[2]
    offsets = weights.shape[0]
    halo = send_rows.shape[2]
    table = slots + 2 * halo
    orders, full = plan(n_space, n_batch)
    steps = 2 * len(orders[0]) + len(full)
    hbm = pl.BlockSpec(memory_space=pltpu.HBM)
    vmem = pl.BlockSpec(memory_space=pltpu.VMEM)
    smem = pl.BlockSpec(memory_space=pltpu.SMEM)
    scale = float((slots * n_space * n_batch) ** -0.5)
    result, grad_features, grad_weights = pl.pallas_call(
        functools.partial(kernel, n_space, n_batch, scale),
        out_shape=(
            jax.ShapeDtypeStruct((slots, channels), BF16),
            jax.ShapeDtypeStruct((slots, channels), BF16),
            jax.ShapeDtypeStruct((offsets, TILES, ROW, channels), F32),
        ),
        in_specs=[hbm, hbm, hbm, hbm, smem, hbm],
        out_specs=(vmem, vmem, vmem),
        scratch_shapes=[
            pltpu.VMEM((slots, channels), BF16),
            pltpu.VMEM((offsets, channels, channels), BF16),
            pltpu.VMEM((offsets, 1, slots), jnp.int32),
            pltpu.VMEM((2, halo), jnp.int32),
            pltpu.VMEM((slots, channels), BF16),
            pltpu.SemaphoreType.DMA((5,)),
            pltpu.VMEM((table, channels), BF16),
            pltpu.VMEM((2 * halo, channels), BF16),
            pltpu.VMEM((channels, table), BF16),
            pltpu.VMEM((slots, channels), BF16),
            pltpu.VMEM((offsets * channels, slots), BF16),
            pltpu.VMEM((offsets, TILES, ROW, channels), F32),
            pltpu.VMEM((offsets, TILES + len(full), ROW, channels), F32),
            pltpu.VMEM((table, 2 * channels), F32),
            pltpu.VMEM((table, channels), F32),
            pltpu.VMEM((2 * halo, channels), F32),
            pltpu.VMEM((channels, slots), F32),
            pltpu.SemaphoreType.DMA((2,)),
            pltpu.SemaphoreType.DMA((2,)),
            pltpu.SemaphoreType.DMA((2,)),
            pltpu.SemaphoreType.DMA((2,)),
            pltpu.SemaphoreType.DMA((GROUPS * steps,)),
            pltpu.SemaphoreType.DMA((GROUPS * steps,)),
        ],
        compiler_params=pltpu.CompilerParams(
            collective_id=0, has_side_effects=True, vmem_limit_bytes=63 * 1024 * 1024
        ),
        name="sparse_conv",
    )(features[0], weights, kernel_map.transpose(1, 0, 2), send_rows[0], counts, cotangent[0])
    return (
        result[None],
        grad_features[None],
        grad_weights.reshape(offsets, channels, channels),
    )


def solution(mesh):
    in_specs = (
        P("batch", "space", None),
        P(),
        P("batch", None, "space"),
        P("batch", None, "space"),
        P("batch", "space"),
        P("batch", "space", None),
    )
    out_specs = (P("batch", "space", None), P("batch", "space", None), P())
    body = functools.partial(per_device, mesh.shape["space"], mesh.shape["batch"])
    return jax.shard_map(body, mesh=mesh, in_specs=in_specs, out_specs=out_specs, check_vma=False)
```

```python
import functools

import jax
import jax.numpy as jnp
from jax import lax
from jax.experimental import pallas as pl
from jax.experimental.pallas import tpu as pltpu
from jax.sharding import PartitionSpec as P

F32 = jnp.float32
BF16 = jnp.bfloat16
MESH = pl.DeviceIdType.MESH
BATCH = 3
SIZES = (8, 8, 8, 4)
FIRSTS = (0, 8, 16, 24)
ROUNDED = 28
GROUPS = len(SIZES)
EARLY = 1
TILES = 16
ROW = 8


def dot(a, b, contract=((1,), (0,))):
    return lax.dot_general(a, b, (contract, ((), ())), preferred_element_type=F32)


def onehot_columns(row, height):
    line = lax.broadcasted_iota(jnp.int16, (height, row.shape[1]), 0)
    hit = line == jnp.broadcast_to(row.astype(jnp.int16), line.shape)
    return jnp.where(hit, jnp.ones((), BF16), jnp.zeros((), BF16))


def split_pair(x):
    high = x.astype(BF16)
    low = (x - high.astype(F32)).astype(BF16)
    return jnp.concatenate([high, low], 1)


def mesh_bits(n_space, n_batch):
    bits = [("batch", 1)] if n_batch > 1 else []
    weight = 1
    while weight < n_space:
        bits.append(("space", weight))
        weight *= 2
    weight = 2
    while weight < n_batch:
        bits.append(("batch", weight))
        weight *= 2
    return bits


def plan(n_space, n_batch):
    bits = mesh_bits(n_space, n_batch)
    return [bits[:1], bits[1:3], bits[3:5]] + [[bit] for bit in bits[5:]]


def kernel(
    n_space, n_batch, scale,
    feat_hbm, w_hbm, kmap_hbm, send_hbm, count, cot_hbm,
    out, gfeat, gw,
    feat, w, kmap, send, cot, load_sem,
    ext, outgoing, extt, grad, gt, dw, inbox0, inbox1, inbox2, inbox3, acc, gext, back, outt,
    halo_send, halo_recv, back_send, back_recv, sum_send, sum_recv,
):
    offsets, channels = w.shape[0], w.shape[1]
    slots = feat.shape[0]
    halo = send.shape[1]
    table = slots + 2 * halo
    here = {"space": lax.axis_index("space"), "batch": lax.axis_index("batch")}
    s = here["space"]
    levels = plan(n_space, n_batch)

    def bit_of(bit):
        return (here[bit[0]] // bit[1]) % 2

    def member(level, flip=0):
        place = 0
        for n, bit in enumerate(levels[level]):
            value = bit_of(bit)
            place = place + (1 - value if flip >> n & 1 else value) * (1 << n)
        return place

    def peer(level, flip):
        there = dict(here)
        for n, bit in enumerate(levels[level]):
            if flip >> n & 1:
                there[bit[0]] = there[bit[0]] + bit[1] * (1 - 2 * bit_of(bit))
        return there

    def flips(level):
        return range(1, 1 << len(levels[level]))

    lower = {**here, "space": s - 1}
    upper = {**here, "space": s + 1}
    has_lower = s > 0
    has_upper = s < n_space - 1

    loads = {}
    pairs = dict(feat=(feat_hbm, feat), send=(send_hbm, send), cot=(cot_hbm, cot), kmap=(kmap_hbm, kmap), w=(w_hbm, w))
    for n, (name, (src, dst)) in enumerate(pairs.items()):
        loads[name] = pltpu.make_async_copy(src, dst, load_sem.at[n])
        loads[name].start()

    barrier = pltpu.get_barrier_semaphore()
    greeted = 0
    for level in range(len(levels)):
        for flip in flips(level):
            pl.semaphore_signal(barrier, inc=1, device_id=peer(level, flip), device_id_type=MESH)
            greeted += 1

    @pl.when(has_lower)
    def _():
        pl.semaphore_signal(barrier, inc=1, device_id=lower, device_id_type=MESH)

    @pl.when(has_upper)
    def _():
        pl.semaphore_signal(barrier, inc=1, device_id=upper, device_id_type=MESH)

    alive = lax.broadcasted_iota(jnp.int32, (slots, channels), 0) < count[0, 0]
    loads["feat"].wait()
    live = jnp.where(alive, feat[...].astype(F32), jnp.zeros((), F32)).astype(BF16)
    ext[:slots] = live
    loads["send"].wait()
    lists = jnp.concatenate([send[0:1, :], send[1:2, :]], 1)
    outgoing[...] = dot(onehot_columns(lists, slots), live, ((0,), (0,))).astype(BF16)

    @pl.when(s == 0)
    def _():
        ext[slots : slots + halo] = jnp.zeros((halo, channels), BF16)
        back[halo:] = jnp.zeros((halo, channels), F32)

    @pl.when(s == n_space - 1)
    def _():
        ext[slots + halo :] = jnp.zeros((halo, channels), BF16)
        back[:halo] = jnp.zeros((halo, channels), F32)

    neighbours = jnp.minimum(s, 1) + jnp.minimum(n_space - 1 - s, 1)
    pl.semaphore_wait(barrier, greeted + neighbours)

    to_lower = pltpu.make_async_remote_copy(
        src_ref=outgoing.at[:halo], dst_ref=ext.at[pl.ds(slots + halo, halo)],
        send_sem=halo_send.at[0], recv_sem=halo_recv.at[0], device_id=lower, device_id_type=MESH)
    to_upper = pltpu.make_async_remote_copy(
        src_ref=outgoing.at[pl.ds(halo, halo)], dst_ref=ext.at[pl.ds(slots, halo)],
        send_sem=halo_send.at[1], recv_sem=halo_recv.at[1], device_id=upper, device_id_type=MESH)

    def start_both(down, up):
        @pl.when(has_lower)
        def _():
            down.start()

        @pl.when(has_upper)
        def _():
            up.start()

    def wait_both(down, up):
        @pl.when(has_lower)
        def _():
            down.wait_send()
            up.wait_recv()

        @pl.when(has_upper)
        def _():
            up.wait_send()
            down.wait_recv()

    start_both(to_lower, to_upper)

    half, part = TILES // 2, TILES // 8
    half_at = member(0) * half
    part_at = half_at + member(1) * part
    steps = len(levels) + 3
    place = [0] * GROUPS
    flying = [()] * GROUPS

    def offsets_of(q, flip=0):
        quarter = SIZES[q] // 4
        return pl.ds(FIRSTS[q] + member(2, flip) * quarter, quarter)

    def launch(q):
        step = place[q]
        group = pl.ds(FIRSTS[q], SIZES[q])
        quarters = pl.ds(FIRSTS[q] // 4, SIZES[q] // 4)
        level = step if step < len(levels) else steps - 1 - step
        copies = []
        for flip in flips(level):
            if step == 0:
                src = dw.at[group, pl.ds(member(0, flip) * half, half)]
                dst = inbox0.at[group]
            elif step == 1:
                src = dw.at[group, pl.ds(half_at + member(1, flip) * part, part)]
                dst = inbox1.at[flip - 1, group]
            elif step == 2:
                src = dw.at[offsets_of(q, flip), pl.ds(part_at, part)]
                dst = inbox2.at[flip - 1, quarters]
            elif step < len(levels):
                src = dw.at[offsets_of(q), pl.ds(part_at, part)]
                dst = inbox3.at[step - 3, quarters]
            else:
                tiles = pl.ds(half_at, half) if level == 0 else pl.ds(part_at, part)
                src = gw.at[offsets_of(q) if level == 2 else group, tiles]
                dst = src
            sem = (q * steps + step) * 3 + flip - 1
            copies.append(pltpu.make_async_remote_copy(
                src_ref=src, dst_ref=dst, send_sem=sum_send.at[sem], recv_sem=sum_recv.at[sem],
                device_id=peer(level, flip), device_id_type=MESH))
            copies[-1].start()
        flying[q] = copies

    def advance(q):
        step = place[q]
        if step >= steps:
            return
        for copy in flying[q]:
            copy.wait()
        group = pl.ds(FIRSTS[q], SIZES[q])
        quarters = pl.ds(FIRSTS[q] // 4, SIZES[q] // 4)
        if step < len(levels):
            if step == 0:
                mine = (group, pl.ds(half_at, half))
                total = dw[mine] + inbox0[group]
            elif step == 1:
                mine = (group, pl.ds(part_at, part))
                total = (dw[mine] + inbox1[0, group]) + (inbox1[1, group] + inbox1[2, group])
            else:
                mine = (offsets_of(q), pl.ds(part_at, part))
                if step == 2:
                    total = (dw[mine] + inbox2[0, quarters]) + (inbox2[1, quarters] + inbox2[2, quarters])
                else:
                    total = dw[mine] + inbox3[step - 3, quarters]
            if step == len(levels) - 1:
                gw[mine] = total * scale
            else:
                dw[mine] = total
        place[q] = step + 1
        if place[q] < steps:
            launch(q)

    def advance_all():
        for q in range(GROUPS):
            advance(q)

    acc[...] = jnp.zeros_like(acc)
    outt[...] = jnp.zeros_like(outt)
    loads["cot"].wait()
    grad[...] = jnp.where(alive, cot[...].astype(F32), jnp.zeros((), F32)).astype(BF16)
    loads["kmap"].wait()
    loads["w"].wait()
    def scatter_step(j, carry):
        weights = w[pl.ds(j * BATCH, BATCH)].reshape(BATCH * channels, channels)
        contrib = dot(grad[...], weights, ((1,), (1,)))
        picks, parts = [], []
        for t in range(BATCH):
            picks.append(onehot_columns(kmap[j * BATCH + t], table))
            parts.append(split_pair(contrib[:, t * channels : (t + 1) * channels]))
        acc[...] += dot(jnp.concatenate(picks, 1), jnp.concatenate(parts, 0))
        return carry

    lax.fori_loop(0, EARLY, scatter_step, 0)
    wait_both(to_lower, to_upper)
    extt[...] = ext[...].astype(F32).T.astype(BF16)

    def weight_step(j, carry):
        for t in range(BATCH):
            k = j * BATCH + t
            picked = onehot_columns(kmap[k], table)
            gathered = dot(extt[...], picked).astype(BF16)
            gt[pl.ds(pl.multiple_of(k * channels, channels), channels)] = gathered
            dw[k] = dot(gathered, grad[...]).reshape(TILES, ROW, channels)
        return carry

    def forward_step(j, carry):
        weights = w[pl.ds(j * BATCH, BATCH)].reshape(BATCH * channels, channels)
        size = BATCH * channels
        rows = gt[pl.ds(pl.multiple_of(j * size, size), size)]
        outt[...] += dot(weights, rows, ((0,), (0,)))
        return carry

    total_loops = offsets // BATCH
    dw[offsets:] = jnp.zeros((ROUNDED - offsets, TILES, ROW, channels), F32)
    lax.fori_loop(0, 3, weight_step, 0)
    launch(0)
    lax.fori_loop(3, 4, weight_step, 0)
    advance(0)
    lax.fori_loop(4, 6, weight_step, 0)
    launch(1)
    lax.fori_loop(6, 7, weight_step, 0)
    advance(0)
    advance(1)
    lax.fori_loop(7, 8, weight_step, 0)
    launch(2)
    lax.fori_loop(8, total_loops, weight_step, 0)
    launch(3)
    lax.fori_loop(EARLY, 2, scatter_step, 0)
    advance_all()
    for j in range(2, total_loops, 2):
        lax.fori_loop(j, min(j + 2, total_loops), scatter_step, 0)
        advance_all()

    both = acc[...]
    gext[...] = both[:, :channels] + both[:, channels:]
    back_lower = pltpu.make_async_remote_copy(
        src_ref=gext.at[pl.ds(slots, halo)], dst_ref=back.at[:halo],
        send_sem=back_send.at[0], recv_sem=back_recv.at[0], device_id=lower, device_id_type=MESH)
    back_upper = pltpu.make_async_remote_copy(
        src_ref=gext.at[pl.ds(slots + halo, halo)], dst_ref=back.at[pl.ds(halo, halo)],
        send_sem=back_send.at[1], recv_sem=back_recv.at[1], device_id=upper, device_id_type=MESH)
    start_both(back_lower, back_upper)

    lax.fori_loop(0, total_loops, forward_step, 0)
    advance_all()
    out[...] = jnp.where(alive, outt[...].T, jnp.zeros((), F32)).astype(BF16)

    wait_both(back_lower, back_upper)
    lists = jnp.concatenate([send[1:2, :], send[0:1, :]], 1)
    extra = dot(onehot_columns(lists, slots), split_pair(back[...]))
    local = gext[:slots] + extra[:, :channels] + extra[:, channels:]
    gfeat[...] = jnp.where(alive, local, jnp.zeros((), F32)).astype(BF16)

    while min(place) < steps:
        advance_all()


def per_device(n_space, n_batch, features, weights, kernel_map, send_rows, counts, cotangent):
    slots, channels = features.shape[1], features.shape[2]
    offsets = weights.shape[0]
    halo = send_rows.shape[2]
    table = slots + 2 * halo
    levels = len(plan(n_space, n_batch))
    steps = levels + 3
    hbm = pl.BlockSpec(memory_space=pltpu.HBM)
    vmem = pl.BlockSpec(memory_space=pltpu.VMEM)
    smem = pl.BlockSpec(memory_space=pltpu.SMEM)
    scale = float((slots * n_space * n_batch) ** -0.5)
    result, grad_features, grad_weights = pl.pallas_call(
        functools.partial(kernel, n_space, n_batch, scale),
        out_shape=(
            jax.ShapeDtypeStruct((slots, channels), BF16),
            jax.ShapeDtypeStruct((slots, channels), BF16),
            jax.ShapeDtypeStruct((ROUNDED, TILES, ROW, channels), F32),
        ),
        in_specs=[hbm, hbm, hbm, hbm, smem, hbm],
        out_specs=(vmem, vmem, vmem),
        scratch_shapes=[
            pltpu.VMEM((slots, channels), BF16),
            pltpu.VMEM((offsets, channels, channels), BF16),
            pltpu.VMEM((offsets, 1, slots), jnp.int32),
            pltpu.VMEM((2, halo), jnp.int32),
            pltpu.VMEM((slots, channels), BF16),
            pltpu.SemaphoreType.DMA((5,)),
            pltpu.VMEM((table, channels), BF16),
            pltpu.VMEM((2 * halo, channels), BF16),
            pltpu.VMEM((channels, table), BF16),
            pltpu.VMEM((slots, channels), BF16),
            pltpu.VMEM((offsets * channels, slots), BF16),
            pltpu.VMEM((ROUNDED, TILES, ROW, channels), F32),
            pltpu.VMEM((ROUNDED, TILES // 2, ROW, channels), F32),
            pltpu.VMEM((3, ROUNDED, TILES // 8, ROW, channels), F32),
            pltpu.VMEM((3, ROUNDED // 4, TILES // 8, ROW, channels), F32),
            pltpu.VMEM((max(levels - 3, 1), ROUNDED // 4, TILES // 8, ROW, channels), F32),
            pltpu.VMEM((table, 2 * channels), F32),
            pltpu.VMEM((table, channels), F32),
            pltpu.VMEM((2 * halo, channels), F32),
            pltpu.VMEM((channels, slots), F32),
            pltpu.SemaphoreType.DMA((2,)),
            pltpu.SemaphoreType.DMA((2,)),
            pltpu.SemaphoreType.DMA((2,)),
            pltpu.SemaphoreType.DMA((2,)),
            pltpu.SemaphoreType.DMA((GROUPS * steps * 3,)),
            pltpu.SemaphoreType.DMA((GROUPS * steps * 3,)),
        ],
        compiler_params=pltpu.CompilerParams(
            collective_id=0, has_side_effects=True, vmem_limit_bytes=48 * 1024 * 1024
        ),
        name="sparse_conv",
    )(*[pltpu.with_memory_space_constraint(v, pltpu.HBM) for v in (features[0], weights, kernel_map.transpose(1, 0, 2), send_rows[0])], counts, pltpu.with_memory_space_constraint(cotangent[0], pltpu.HBM))
    return (
        result[None],
        grad_features[None],
        grad_weights[:offsets].reshape(offsets, channels, channels),
    )


def solution(mesh):
    in_specs = (
        P("batch", "space", None),
        P(),
        P("batch", None, "space"),
        P("batch", None, "space"),
        P("batch", "space"),
        P("batch", "space", None),
    )
    out_specs = (P("batch", "space", None), P("batch", "space", None), P())
    body = functools.partial(per_device, mesh.shape["space"], mesh.shape["batch"])
    return jax.shard_map(body, mesh=mesh, in_specs=in_specs, out_specs=out_specs, check_vma=False)
```

```python
import functools

import jax
import jax.numpy as jnp
from jax import lax
from jax.experimental import pallas as pl
from jax.experimental.pallas import tpu as pltpu
from jax.sharding import PartitionSpec as P

F32 = jnp.float32
BF16 = jnp.bfloat16
MESH = pl.DeviceIdType.MESH
BATCH = 3
SIZES = (8, 8, 8, 4)
FIRSTS = (0, 8, 16, 24)
ROUNDED = 28
GROUPS = len(SIZES)
EARLY = 1
TILES = 16
ROW = 8


def dot(a, b, contract=((1,), (0,))):
    return lax.dot_general(a, b, (contract, ((), ())), preferred_element_type=F32)


def onehot_columns(row, height):
    line = lax.broadcasted_iota(jnp.int16, (height, row.shape[1]), 0)
    hit = line == jnp.broadcast_to(row.astype(jnp.int16), line.shape)
    return jnp.where(hit, jnp.ones((), BF16), jnp.zeros((), BF16))


def split_pair(x):
    high = x.astype(BF16)
    low = (x - high.astype(F32)).astype(BF16)
    return jnp.concatenate([high, low], 1)


def mesh_bits(n_space, n_batch):
    bits = [("batch", 1)] if n_batch > 1 else []
    weight = 1
    while weight < n_space:
        bits.append(("space", weight))
        weight *= 2
    weight = 2
    while weight < n_batch:
        bits.append(("batch", weight))
        weight *= 2
    return bits


def plan(n_space, n_batch):
    bits = mesh_bits(n_space, n_batch)
    return [bits[:1], bits[1:3], bits[3:5]] + [[bit] for bit in bits[5:]]


def kernel(
    n_space, n_batch, scale,
    feat_hbm, w_hbm, kmap_hbm, send_hbm, count, cot_hbm,
    out, gfeat, gw,
    feat, w, kmap, send, cot, load_sem,
    ext, outgoing, extt, grad, gt, dw, inbox0, inbox1, inbox2, inbox3, acc, gext, back, outt,
    halo_send, halo_recv, back_send, back_recv, sum_send, sum_recv,
):
    offsets, channels = w.shape[0], w.shape[1]
    slots = feat.shape[0]
    halo = send.shape[1]
    table = slots + 2 * halo
    here = {"space": lax.axis_index("space"), "batch": lax.axis_index("batch")}
    s = here["space"]
    levels = plan(n_space, n_batch)

    def bit_of(bit):
        return (here[bit[0]] // bit[1]) % 2

    def member(level, flip=0):
        place = 0
        for n, bit in enumerate(levels[level]):
            value = bit_of(bit)
            place = place + (1 - value if flip >> n & 1 else value) * (1 << n)
        return place

    def peer(level, flip):
        there = dict(here)
        for n, bit in enumerate(levels[level]):
            if flip >> n & 1:
                there[bit[0]] = there[bit[0]] + bit[1] * (1 - 2 * bit_of(bit))
        return there

    def flips(level):
        return range(1, 1 << len(levels[level]))

    lower = {**here, "space": s - 1}
    upper = {**here, "space": s + 1}
    has_lower = s > 0
    has_upper = s < n_space - 1

    loads = {}
    pairs = dict(feat=(feat_hbm, feat), send=(send_hbm, send), cot=(cot_hbm, cot), kmap=(kmap_hbm, kmap), w=(w_hbm, w))
    for n, (name, (src, dst)) in enumerate(pairs.items()):
        loads[name] = pltpu.make_async_copy(src, dst, load_sem.at[n])
        loads[name].start()

    barrier = pltpu.get_barrier_semaphore()
    greeted = 0
    for level in range(len(levels)):
        for flip in flips(level):
            pl.semaphore_signal(barrier, inc=1, device_id=peer(level, flip), device_id_type=MESH)
            greeted += 1

    @pl.when(has_lower)
    def _():
        pl.semaphore_signal(barrier, inc=1, device_id=lower, device_id_type=MESH)

    @pl.when(has_upper)
    def _():
        pl.semaphore_signal(barrier, inc=1, device_id=upper, device_id_type=MESH)

    alive = lax.broadcasted_iota(jnp.int32, (slots, channels), 0) < count[0, 0]
    loads["feat"].wait()
    live = jnp.where(alive, feat[...].astype(F32), jnp.zeros((), F32)).astype(BF16)
    ext[:slots] = live
    loads["send"].wait()
    lists = jnp.concatenate([send[0:1, :], send[1:2, :]], 1)
    outgoing[...] = dot(onehot_columns(lists, slots), live, ((0,), (0,))).astype(BF16)

    @pl.when(s == 0)
    def _():
        ext[slots : slots + halo] = jnp.zeros((halo, channels), BF16)
        back[halo:] = jnp.zeros((halo, channels), F32)

    @pl.when(s == n_space - 1)
    def _():
        ext[slots + halo :] = jnp.zeros((halo, channels), BF16)
        back[:halo] = jnp.zeros((halo, channels), F32)

    neighbours = jnp.minimum(s, 1) + jnp.minimum(n_space - 1 - s, 1)
    pl.semaphore_wait(barrier, greeted + neighbours)

    to_lower = pltpu.make_async_remote_copy(
        src_ref=outgoing.at[:halo], dst_ref=ext.at[pl.ds(slots + halo, halo)],
        send_sem=halo_send.at[0], recv_sem=halo_recv.at[0], device_id=lower, device_id_type=MESH)
    to_upper = pltpu.make_async_remote_copy(
        src_ref=outgoing.at[pl.ds(halo, halo)], dst_ref=ext.at[pl.ds(slots, halo)],
        send_sem=halo_send.at[1], recv_sem=halo_recv.at[1], device_id=upper, device_id_type=MESH)

    def start_both(down, up):
        @pl.when(has_lower)
        def _():
            down.start()

        @pl.when(has_upper)
        def _():
            up.start()

    def wait_both(down, up):
        @pl.when(has_lower)
        def _():
            down.wait_send()
            up.wait_recv()

        @pl.when(has_upper)
        def _():
            up.wait_send()
            down.wait_recv()

    start_both(to_lower, to_upper)

    half, part = TILES // 2, TILES // 8
    half_at = member(0) * half
    part_at = half_at + member(1) * part
    steps = len(levels) + 3
    place = [0] * GROUPS

    def offsets_of(q, flip=0):
        quarter = SIZES[q] // 4
        return pl.ds(FIRSTS[q] + member(2, flip) * quarter, quarter)

    def copies_of(q):
        step = place[q]
        group = pl.ds(FIRSTS[q], SIZES[q])
        quarters = pl.ds(FIRSTS[q] // 4, SIZES[q] // 4)
        level = step if step < len(levels) else steps - 1 - step
        copies = []
        for flip in flips(level):
            if step == 0:
                src = dw.at[group, pl.ds(member(0, flip) * half, half)]
                dst = inbox0.at[group]
            elif step == 1:
                src = dw.at[group, pl.ds(half_at + member(1, flip) * part, part)]
                dst = inbox1.at[flip - 1, group]
            elif step == 2:
                src = dw.at[offsets_of(q, flip), pl.ds(part_at, part)]
                dst = inbox2.at[flip - 1, quarters]
            elif step < len(levels):
                src = dw.at[offsets_of(q), pl.ds(part_at, part)]
                dst = inbox3.at[step - 3, quarters]
            else:
                tiles = pl.ds(half_at, half) if level == 0 else pl.ds(part_at, part)
                src = gw.at[offsets_of(q) if level == 2 else group, tiles]
                dst = src
            sem = (q * steps + step) * 3 + flip - 1
            copies.append(pltpu.make_async_remote_copy(
                src_ref=src, dst_ref=dst, send_sem=sum_send.at[sem], recv_sem=sum_recv.at[sem],
                device_id=peer(level, flip), device_id_type=MESH))
        return copies

    def launch(q):
        for copy in copies_of(q):
            copy.start()

    def advance(q):
        step = place[q]
        if step >= steps:
            return
        for copy in copies_of(q):
            copy.wait()
        group = pl.ds(FIRSTS[q], SIZES[q])
        quarters = pl.ds(FIRSTS[q] // 4, SIZES[q] // 4)
        if step < len(levels):
            if step == 0:
                mine = (group, pl.ds(half_at, half))
                total = dw[mine] + inbox0[group]
            elif step == 1:
                mine = (group, pl.ds(part_at, part))
                total = (dw[mine] + inbox1[0, group]) + (inbox1[1, group] + inbox1[2, group])
            else:
                mine = (offsets_of(q), pl.ds(part_at, part))
                if step == 2:
                    total = (dw[mine] + inbox2[0, quarters]) + (inbox2[1, quarters] + inbox2[2, quarters])
                else:
                    total = dw[mine] + inbox3[step - 3, quarters]
            if step == len(levels) - 1:
                gw[mine] = total * scale
            else:
                dw[mine] = total
        place[q] = step + 1
        if place[q] < steps:
            launch(q)

    def advance_all():
        for q in range(GROUPS):
            advance(q)

    acc[...] = jnp.zeros_like(acc)
    outt[...] = jnp.zeros_like(outt)
    loads["cot"].wait()
    grad[...] = jnp.where(alive, cot[...].astype(F32), jnp.zeros((), F32)).astype(BF16)
    loads["kmap"].wait()
    loads["w"].wait()
    def scatter_step(j, carry):
        weights = w[pl.ds(j * BATCH, BATCH)].reshape(BATCH * channels, channels)
        contrib = dot(grad[...], weights, ((1,), (1,)))
        picks, parts = [], []
        for t in range(BATCH):
            picks.append(onehot_columns(kmap[j * BATCH + t], table))
            parts.append(split_pair(contrib[:, t * channels : (t + 1) * channels]))
        acc[...] += dot(jnp.concatenate(picks, 1), jnp.concatenate(parts, 0))
        return carry

    scatter_step(0, 0)
    wait_both(to_lower, to_upper)
    extt[...] = ext[...].astype(F32).T.astype(BF16)

    def weight_step(j, carry):
        for t in range(BATCH):
            k = j * BATCH + t
            picked = onehot_columns(kmap[k], table)
            gathered = dot(extt[...], picked).astype(BF16)
            gt[pl.ds(pl.multiple_of(k * channels, channels), channels)] = gathered
            dw[k] = dot(gathered, grad[...]).reshape(TILES, ROW, channels)
        return carry

    def forward_step(j, carry):
        weights = w[pl.ds(j * BATCH, BATCH)].reshape(BATCH * channels, channels)
        size = BATCH * channels
        rows = gt[pl.ds(pl.multiple_of(j * size, size), size)]
        outt[...] += dot(weights, rows, ((0,), (0,)))
        return carry

    total_loops = offsets // BATCH
    dw[offsets:] = jnp.zeros((ROUNDED - offsets, TILES, ROW, channels), F32)

    def after_weights(j):
        @pl.when(j == 2)
        def _():
            launch(0)

        @pl.when(j == 3)
        def _():
            advance(0)

        @pl.when(j == 5)
        def _():
            launch(1)

        @pl.when(j == 6)
        def _():
            advance(0)
            advance(1)

        @pl.when(j == 7)
        def _():
            launch(2)

        @pl.when(j == 8)
        def _():
            launch(3)

    def weight_stage(j, carry):
        weight_step(j, carry)
        after_weights(j)
        return carry

    def scatter_stage(j, carry):
        scatter_step(j, carry)
        forward_step(j, carry)
        for tick in (1, 3, 4, 6, 8):
            pl.when(j == tick)(lambda tick=tick: advance_all())
        return carry

    lax.fori_loop(0, total_loops, weight_stage, 0)
    lax.fori_loop(EARLY, total_loops, scatter_stage, 0)

    both = acc[...]
    gext[...] = both[:, :channels] + both[:, channels:]
    back_lower = pltpu.make_async_remote_copy(
        src_ref=gext.at[pl.ds(slots, halo)], dst_ref=back.at[:halo],
        send_sem=back_send.at[0], recv_sem=back_recv.at[0], device_id=lower, device_id_type=MESH)
    back_upper = pltpu.make_async_remote_copy(
        src_ref=gext.at[pl.ds(slots + halo, halo)], dst_ref=back.at[pl.ds(halo, halo)],
        send_sem=back_send.at[1], recv_sem=back_recv.at[1], device_id=upper, device_id_type=MESH)
    start_both(back_lower, back_upper)

    forward_step(0, 0)
    out[...] = jnp.where(alive, outt[...].T, jnp.zeros((), F32)).astype(BF16)

    wait_both(back_lower, back_upper)
    lists = jnp.concatenate([send[1:2, :], send[0:1, :]], 1)
    extra = dot(onehot_columns(lists, slots), split_pair(back[...]))
    local = gext[:slots] + extra[:, :channels] + extra[:, channels:]
    gfeat[...] = jnp.where(alive, local, jnp.zeros((), F32)).astype(BF16)

    while min(place) < steps:
        advance_all()


def per_device(n_space, n_batch, features, weights, kernel_map, send_rows, counts, cotangent):
    slots, channels = features.shape[1], features.shape[2]
    offsets = weights.shape[0]
    halo = send_rows.shape[2]
    table = slots + 2 * halo
    levels = len(plan(n_space, n_batch))
    steps = levels + 3
    hbm = pl.BlockSpec(memory_space=pltpu.HBM)
    vmem = pl.BlockSpec(memory_space=pltpu.VMEM)
    smem = pl.BlockSpec(memory_space=pltpu.SMEM)
    scale = float((slots * n_space * n_batch) ** -0.5)
    result, grad_features, grad_weights = pl.pallas_call(
        functools.partial(kernel, n_space, n_batch, scale),
        out_shape=(
            jax.ShapeDtypeStruct((slots, channels), BF16),
            jax.ShapeDtypeStruct((slots, channels), BF16),
            jax.ShapeDtypeStruct((ROUNDED, TILES, ROW, channels), F32),
        ),
        in_specs=[hbm, hbm, hbm, hbm, smem, hbm],
        out_specs=(vmem, vmem, vmem),
        scratch_shapes=[
            pltpu.VMEM((slots, channels), BF16),
            pltpu.VMEM((offsets, channels, channels), BF16),
            pltpu.VMEM((offsets, 1, slots), jnp.int32),
            pltpu.VMEM((2, halo), jnp.int32),
            pltpu.VMEM((slots, channels), BF16),
            pltpu.SemaphoreType.DMA((5,)),
            pltpu.VMEM((table, channels), BF16),
            pltpu.VMEM((2 * halo, channels), BF16),
            pltpu.VMEM((channels, table), BF16),
            pltpu.VMEM((slots, channels), BF16),
            pltpu.VMEM((offsets * channels, slots), BF16),
            pltpu.VMEM((ROUNDED, TILES, ROW, channels), F32),
            pltpu.VMEM((ROUNDED, TILES // 2, ROW, channels), F32),
            pltpu.VMEM((3, ROUNDED, TILES // 8, ROW, channels), F32),
            pltpu.VMEM((3, ROUNDED // 4, TILES // 8, ROW, channels), F32),
            pltpu.VMEM((max(levels - 3, 1), ROUNDED // 4, TILES // 8, ROW, channels), F32),
            pltpu.VMEM((table, 2 * channels), F32),
            pltpu.VMEM((table, channels), F32),
            pltpu.VMEM((2 * halo, channels), F32),
            pltpu.VMEM((channels, slots), F32),
            pltpu.SemaphoreType.DMA((2,)),
            pltpu.SemaphoreType.DMA((2,)),
            pltpu.SemaphoreType.DMA((2,)),
            pltpu.SemaphoreType.DMA((2,)),
            pltpu.SemaphoreType.DMA((GROUPS * steps * 3,)),
            pltpu.SemaphoreType.DMA((GROUPS * steps * 3,)),
        ],
        compiler_params=pltpu.CompilerParams(
            collective_id=0, has_side_effects=True, vmem_limit_bytes=48 * 1024 * 1024
        ),
        name="sparse_conv",
    )(*[pltpu.with_memory_space_constraint(v, pltpu.HBM) for v in (features[0], weights, kernel_map.transpose(1, 0, 2), send_rows[0])], counts, pltpu.with_memory_space_constraint(cotangent[0], pltpu.HBM))
    return (
        result[None],
        grad_features[None],
        grad_weights[:offsets].reshape(offsets, channels, channels),
    )


def solution(mesh):
    in_specs = (
        P("batch", "space", None),
        P(),
        P("batch", None, "space"),
        P("batch", None, "space"),
        P("batch", "space"),
        P("batch", "space", None),
    )
    out_specs = (P("batch", "space", None), P("batch", "space", None), P())
    body = functools.partial(per_device, mesh.shape["space"], mesh.shape["batch"])
    return jax.shard_map(body, mesh=mesh, in_specs=in_specs, out_specs=out_specs, check_vma=False)
```

```python
import functools

import jax
import jax.numpy as jnp
from jax import lax
from jax.experimental import pallas as pl
from jax.experimental.pallas import tpu as pltpu
from jax.sharding import PartitionSpec as P

F32 = jnp.float32
BF16 = jnp.bfloat16
MESH = pl.DeviceIdType.MESH
BATCH = 3
SIZES = (8, 8, 8, 4)
FIRSTS = (0, 8, 16, 24)
ROUNDED = 28
GROUPS = len(SIZES)
EARLY = 1
TILES = 16
ROW = 8


def dot(a, b, contract=((1,), (0,))):
    return lax.dot_general(a, b, (contract, ((), ())), preferred_element_type=F32)


def onehot_columns(row, height):
    line = lax.broadcasted_iota(jnp.int16, (height, row.shape[1]), 0)
    hit = line == jnp.broadcast_to(row.astype(jnp.int16), line.shape)
    return jnp.where(hit, jnp.ones((), BF16), jnp.zeros((), BF16))


def split_pair(x):
    high = x.astype(BF16)
    low = (x - high.astype(F32)).astype(BF16)
    return jnp.concatenate([high, low], 1)


def mesh_bits(n_space, n_batch):
    bits = [("batch", 1)] if n_batch > 1 else []
    weight = 1
    while weight < n_space:
        bits.append(("space", weight))
        weight *= 2
    weight = 2
    while weight < n_batch:
        bits.append(("batch", weight))
        weight *= 2
    return bits


def plan(n_space, n_batch):
    bits = mesh_bits(n_space, n_batch)
    return [bits[:1], bits[1:3], bits[3:5]] + [[bit] for bit in bits[5:]]


def kernel(
    n_space, n_batch, scale,
    feat_hbm, w_hbm, kmap_hbm, send_hbm, count, cot_hbm,
    out, gfeat, gw,
    feat, w, kmap, send, cot, load_sem,
    ext, outgoing, extt, grad, gt, dw, inbox0, inbox1, inbox2, inbox3, acc, gext, back, outt,
    halo_send, halo_recv, back_send, back_recv, sum_send, sum_recv,
):
    offsets, channels = w.shape[0], w.shape[1]
    slots = feat.shape[0]
    halo = send.shape[1]
    table = slots + 2 * halo
    here = {"space": lax.axis_index("space"), "batch": lax.axis_index("batch")}
    s = here["space"]
    levels = plan(n_space, n_batch)

    def bit_of(bit):
        return (here[bit[0]] // bit[1]) % 2

    def member(level, flip=0):
        place = 0
        for n, bit in enumerate(levels[level]):
            value = bit_of(bit)
            place = place + (1 - value if flip >> n & 1 else value) * (1 << n)
        return place

    def peer(level, flip):
        there = dict(here)
        for n, bit in enumerate(levels[level]):
            if flip >> n & 1:
                there[bit[0]] = there[bit[0]] + bit[1] * (1 - 2 * bit_of(bit))
        return there

    def flips(level):
        return range(1, 1 << len(levels[level]))

    lower = {**here, "space": s - 1}
    upper = {**here, "space": s + 1}
    has_lower = s > 0
    has_upper = s < n_space - 1

    loads = {}
    pairs = dict(feat=(feat_hbm, feat), send=(send_hbm, send), cot=(cot_hbm, cot), kmap=(kmap_hbm, kmap), w=(w_hbm, w))
    for n, (name, (src, dst)) in enumerate(pairs.items()):
        loads[name] = pltpu.make_async_copy(src, dst, load_sem.at[n])
        loads[name].start()

    barrier = pltpu.get_barrier_semaphore()
    greeted = 0
    for level in range(len(levels)):
        for flip in flips(level):
            pl.semaphore_signal(barrier, inc=1, device_id=peer(level, flip), device_id_type=MESH)
            greeted += 1

    @pl.when(has_lower)
    def _():
        pl.semaphore_signal(barrier, inc=1, device_id=lower, device_id_type=MESH)

    @pl.when(has_upper)
    def _():
        pl.semaphore_signal(barrier, inc=1, device_id=upper, device_id_type=MESH)

    alive = lax.broadcasted_iota(jnp.int32, (slots, channels), 0) < count[0, 0]
    loads["feat"].wait()
    live = jnp.where(alive, feat[...].astype(F32), jnp.zeros((), F32)).astype(BF16)
    ext[:slots] = live
    loads["send"].wait()
    lists = jnp.concatenate([send[0:1, :], send[1:2, :]], 1)
    outgoing[...] = dot(onehot_columns(lists, slots), live, ((0,), (0,))).astype(BF16)

    @pl.when(s == 0)
    def _():
        ext[slots : slots + halo] = jnp.zeros((halo, channels), BF16)
        back[halo:] = jnp.zeros((halo, channels), F32)

    @pl.when(s == n_space - 1)
    def _():
        ext[slots + halo :] = jnp.zeros((halo, channels), BF16)
        back[:halo] = jnp.zeros((halo, channels), F32)

    neighbours = jnp.minimum(s, 1) + jnp.minimum(n_space - 1 - s, 1)
    pl.semaphore_wait(barrier, greeted + neighbours)

    to_lower = pltpu.make_async_remote_copy(
        src_ref=outgoing.at[:halo], dst_ref=ext.at[pl.ds(slots + halo, halo)],
        send_sem=halo_send.at[0], recv_sem=halo_recv.at[0], device_id=lower, device_id_type=MESH)
    to_upper = pltpu.make_async_remote_copy(
        src_ref=outgoing.at[pl.ds(halo, halo)], dst_ref=ext.at[pl.ds(slots, halo)],
        send_sem=halo_send.at[1], recv_sem=halo_recv.at[1], device_id=upper, device_id_type=MESH)

    def start_both(down, up):
        @pl.when(has_lower)
        def _():
            down.start()

        @pl.when(has_upper)
        def _():
            up.start()

    def wait_both(down, up):
        @pl.when(has_lower)
        def _():
            down.wait_send()
            up.wait_recv()

        @pl.when(has_upper)
        def _():
            up.wait_send()
            down.wait_recv()

    start_both(to_lower, to_upper)

    half, part = TILES // 2, TILES // 8
    half_at = member(0) * half
    part_at = half_at + member(1) * part
    steps = len(levels) + 3
    place = [0] * GROUPS

    def offsets_of(q, flip=0):
        quarter = SIZES[q] // 4
        return pl.ds(FIRSTS[q] + member(2, flip) * quarter, quarter)

    def copies_of(q):
        step = place[q]
        group = pl.ds(FIRSTS[q], SIZES[q])
        quarters = pl.ds(FIRSTS[q] // 4, SIZES[q] // 4)
        level = step if step < len(levels) else steps - 1 - step
        copies = []
        for flip in flips(level):
            if step == 0:
                src = dw.at[group, pl.ds(member(0, flip) * half, half)]
                dst = inbox0.at[group]
            elif step == 1:
                src = dw.at[group, pl.ds(half_at + member(1, flip) * part, part)]
                dst = inbox1.at[flip - 1, group]
            elif step == 2:
                src = dw.at[offsets_of(q, flip), pl.ds(part_at, part)]
                dst = inbox2.at[flip - 1, quarters]
            elif step < len(levels):
                src = dw.at[offsets_of(q), pl.ds(part_at, part)]
                dst = inbox3.at[step - 3, quarters]
            else:
                tiles = pl.ds(half_at, half) if level == 0 else pl.ds(part_at, part)
                src = gw.at[offsets_of(q) if level == 2 else group, tiles]
                dst = src
            sem = (q * steps + step) * 3 + flip - 1
            copies.append(pltpu.make_async_remote_copy(
                src_ref=src, dst_ref=dst, send_sem=sum_send.at[sem], recv_sem=sum_recv.at[sem],
                device_id=peer(level, flip), device_id_type=MESH))
        return copies

    def launch(q):
        for copy in copies_of(q):
            copy.start()

    def advance(q):
        step = place[q]
        if step >= steps:
            return
        for copy in copies_of(q):
            copy.wait()
        group = pl.ds(FIRSTS[q], SIZES[q])
        quarters = pl.ds(FIRSTS[q] // 4, SIZES[q] // 4)
        if step < len(levels):
            if step == 0:
                mine = (group, pl.ds(half_at, half))
                total = dw[mine] + inbox0[group]
            elif step == 1:
                mine = (group, pl.ds(part_at, part))
                total = (dw[mine] + inbox1[0, group]) + (inbox1[1, group] + inbox1[2, group])
            else:
                mine = (offsets_of(q), pl.ds(part_at, part))
                if step == 2:
                    total = (dw[mine] + inbox2[0, quarters]) + (inbox2[1, quarters] + inbox2[2, quarters])
                else:
                    total = dw[mine] + inbox3[step - 3, quarters]
            if step == len(levels) - 1:
                gw[mine] = total * scale
            else:
                dw[mine] = total
        place[q] = step + 1
        if place[q] < steps:
            launch(q)

    def advance_all():
        for q in range(GROUPS):
            advance(q)

    acc[...] = jnp.zeros_like(acc)
    outt[...] = jnp.zeros_like(outt)
    loads["cot"].wait()
    grad[...] = jnp.where(alive, cot[...].astype(F32), jnp.zeros((), F32)).astype(BF16)
    loads["kmap"].wait()
    loads["w"].wait()
    def scatter_step(j, carry):
        weights = w[pl.ds(j * BATCH, BATCH)].reshape(BATCH * channels, channels)
        contrib = dot(grad[...], weights, ((1,), (1,)))
        picks, parts = [], []
        for t in range(BATCH):
            picks.append(onehot_columns(kmap[j * BATCH + t], table))
            parts.append(split_pair(contrib[:, t * channels : (t + 1) * channels]))
        acc[...] += dot(jnp.concatenate(picks, 1), jnp.concatenate(parts, 0))
        return carry

    scatter_step(0, 0)
    wait_both(to_lower, to_upper)
    extt[...] = ext[...].astype(F32).T.astype(BF16)

    def weight_step(j, carry):
        size = BATCH * channels
        picks = [onehot_columns(kmap[j * BATCH + t], table) for t in range(BATCH)]
        gathered = jnp.concatenate([dot(extt[...], picked).astype(BF16) for picked in picks], 0)
        gt[pl.ds(pl.multiple_of(j * size, size), size)] = gathered
        products = dot(gathered, grad[...])
        dw[pl.ds(j * BATCH, BATCH)] = products.reshape(BATCH, TILES, ROW, channels)
        return carry

    def forward_step(j, carry):
        weights = w[pl.ds(j * BATCH, BATCH)].reshape(BATCH * channels, channels)
        size = BATCH * channels
        rows = gt[pl.ds(pl.multiple_of(j * size, size), size)]
        outt[...] += dot(weights, rows, ((0,), (0,)))
        return carry

    total_loops = offsets // BATCH
    dw[offsets:] = jnp.zeros((ROUNDED - offsets, TILES, ROW, channels), F32)

    def after_weights(j):
        @pl.when(j == 2)
        def _():
            launch(0)

        @pl.when(j == 3)
        def _():
            advance(0)

        @pl.when(j == 5)
        def _():
            launch(1)

        @pl.when(j == 6)
        def _():
            advance(0)
            advance(1)

        @pl.when(j == 7)
        def _():
            launch(2)

        @pl.when(j == 8)
        def _():
            launch(3)

    def weight_stage(j, carry):
        weight_step(j, carry)
        after_weights(j)
        return carry

    def scatter_stage(ticks, forward):
        def stage(j, carry):
            scatter_step(j, carry)
            if forward:
                forward_step(j, carry)
            for tick in ticks:
                pl.when(j == tick)(lambda tick=tick: advance_all())
            return carry

        return stage

    late = 2 * total_loops // 3
    lax.fori_loop(0, total_loops, weight_stage, 0)
    forward_step(0, 0)
    lax.fori_loop(EARLY, late, scatter_stage((1, 3, 4), True), 0)
    lax.fori_loop(late, total_loops, scatter_stage((6, 8), False), 0)

    both = acc[...]
    gext[...] = both[:, :channels] + both[:, channels:]
    back_lower = pltpu.make_async_remote_copy(
        src_ref=gext.at[pl.ds(slots, halo)], dst_ref=back.at[:halo],
        send_sem=back_send.at[0], recv_sem=back_recv.at[0], device_id=lower, device_id_type=MESH)
    back_upper = pltpu.make_async_remote_copy(
        src_ref=gext.at[pl.ds(slots + halo, halo)], dst_ref=back.at[pl.ds(halo, halo)],
        send_sem=back_send.at[1], recv_sem=back_recv.at[1], device_id=upper, device_id_type=MESH)
    start_both(back_lower, back_upper)

    lax.fori_loop(late, total_loops, forward_step, 0)
    out[...] = jnp.where(alive, outt[...].T, jnp.zeros((), F32)).astype(BF16)

    wait_both(back_lower, back_upper)
    lists = jnp.concatenate([send[1:2, :], send[0:1, :]], 1)
    extra = dot(onehot_columns(lists, slots), split_pair(back[...]))
    local = gext[:slots] + extra[:, :channels] + extra[:, channels:]
    gfeat[...] = jnp.where(alive, local, jnp.zeros((), F32)).astype(BF16)

    while min(place) < steps:
        advance_all()


def per_device(n_space, n_batch, features, weights, kernel_map, send_rows, counts, cotangent):
    slots, channels = features.shape[1], features.shape[2]
    offsets = weights.shape[0]
    halo = send_rows.shape[2]
    table = slots + 2 * halo
    levels = len(plan(n_space, n_batch))
    steps = levels + 3
    hbm = pl.BlockSpec(memory_space=pltpu.HBM)
    vmem = pl.BlockSpec(memory_space=pltpu.VMEM)
    smem = pl.BlockSpec(memory_space=pltpu.SMEM)
    scale = float((slots * n_space * n_batch) ** -0.5)
    result, grad_features, grad_weights = pl.pallas_call(
        functools.partial(kernel, n_space, n_batch, scale),
        out_shape=(
            jax.ShapeDtypeStruct((slots, channels), BF16),
            jax.ShapeDtypeStruct((slots, channels), BF16),
            jax.ShapeDtypeStruct((ROUNDED, TILES, ROW, channels), F32),
        ),
        in_specs=[hbm, hbm, hbm, hbm, smem, hbm],
        out_specs=(vmem, vmem, vmem),
        scratch_shapes=[
            pltpu.VMEM((slots, channels), BF16),
            pltpu.VMEM((offsets, channels, channels), BF16),
            pltpu.VMEM((offsets, 1, slots), jnp.int32),
            pltpu.VMEM((2, halo), jnp.int32),
            pltpu.VMEM((slots, channels), BF16),
            pltpu.SemaphoreType.DMA((5,)),
            pltpu.VMEM((table, channels), BF16),
            pltpu.VMEM((2 * halo, channels), BF16),
            pltpu.VMEM((channels, table), BF16),
            pltpu.VMEM((slots, channels), BF16),
            pltpu.VMEM((offsets * channels, slots), BF16),
            pltpu.VMEM((ROUNDED, TILES, ROW, channels), F32),
            pltpu.VMEM((ROUNDED, TILES // 2, ROW, channels), F32),
            pltpu.VMEM((3, ROUNDED, TILES // 8, ROW, channels), F32),
            pltpu.VMEM((3, ROUNDED // 4, TILES // 8, ROW, channels), F32),
            pltpu.VMEM((max(levels - 3, 1), ROUNDED // 4, TILES // 8, ROW, channels), F32),
            pltpu.VMEM((table, 2 * channels), F32),
            pltpu.VMEM((table, channels), F32),
            pltpu.VMEM((2 * halo, channels), F32),
            pltpu.VMEM((channels, slots), F32),
            pltpu.SemaphoreType.DMA((2,)),
            pltpu.SemaphoreType.DMA((2,)),
            pltpu.SemaphoreType.DMA((2,)),
            pltpu.SemaphoreType.DMA((2,)),
            pltpu.SemaphoreType.DMA((GROUPS * steps * 3,)),
            pltpu.SemaphoreType.DMA((GROUPS * steps * 3,)),
        ],
        compiler_params=pltpu.CompilerParams(
            collective_id=0, has_side_effects=True, vmem_limit_bytes=48 * 1024 * 1024
        ),
        name="sparse_conv",
    )(*[pltpu.with_memory_space_constraint(v, pltpu.HBM) for v in (features[0], weights, kernel_map.transpose(1, 0, 2), send_rows[0])], counts, pltpu.with_memory_space_constraint(cotangent[0], pltpu.HBM))
    return (
        result[None],
        grad_features[None],
        grad_weights[:offsets].reshape(offsets, channels, channels),
    )


def solution(mesh):
    in_specs = (
        P("batch", "space", None),
        P(),
        P("batch", None, "space"),
        P("batch", None, "space"),
        P("batch", "space"),
        P("batch", "space", None),
    )
    out_specs = (P("batch", "space", None), P("batch", "space", None), P())
    body = functools.partial(per_device, mesh.shape["space"], mesh.shape["batch"])
    return jax.shard_map(body, mesh=mesh, in_specs=in_specs, out_specs=out_specs, check_vma=False)
```

```python
import functools

import jax
import jax.numpy as jnp
from jax import lax
from jax.experimental import pallas as pl
from jax.experimental.pallas import tpu as pltpu
from jax.sharding import PartitionSpec as P

F32 = jnp.float32
BF16 = jnp.bfloat16
MESH = pl.DeviceIdType.MESH
BATCH = 3
SIZES = (8, 8, 8, 4)
FIRSTS = (0, 8, 16, 24)
ROUNDED = 28
GROUPS = len(SIZES)
EARLY = 1
TILES = 16
ROW = 8
LANES = 128


def dot(a, b, contract=((1,), (0,))):
    return lax.dot_general(a, b, (contract, ((), ())), preferred_element_type=F32)


def onehot_columns(row, lines):
    lines = lines[...]
    row = row.astype(jnp.int16)
    blocks = []
    for at in range(0, row.shape[1], LANES):
        hit = lines == jnp.broadcast_to(row[:, at : at + LANES], lines.shape)
        blocks.append(jnp.where(hit, jnp.ones((), BF16), jnp.zeros((), BF16)))
    return jnp.concatenate(blocks, 1)


def split_pair(x):
    high = x.astype(BF16)
    low = (x - high.astype(F32)).astype(BF16)
    return jnp.concatenate([high, low], 1)


def mesh_bits(n_space, n_batch):
    bits = [("batch", 1)] if n_batch > 1 else []
    weight = 1
    while weight < n_space:
        bits.append(("space", weight))
        weight *= 2
    weight = 2
    while weight < n_batch:
        bits.append(("batch", weight))
        weight *= 2
    return bits


def plan(n_space, n_batch):
    bits = mesh_bits(n_space, n_batch)
    return [bits[:1], bits[1:3], bits[3:5]] + [[bit] for bit in bits[5:]]


def kernel(
    n_space, n_batch, scale,
    feat_hbm, w_hbm, kmap_hbm, send_hbm, count, cot_hbm,
    out, gfeat, gw,
    feat, w, kmap, send, cot, load_sem, lines,
    ext, outgoing, extt, grad, gt, dw, inbox0, inbox1, inbox2, inbox3, acc, gext, back, outt,
    halo_send, halo_recv, back_send, back_recv, sum_send, sum_recv,
):
    offsets, channels = w.shape[0], w.shape[1]
    slots = feat.shape[0]
    halo = send.shape[1]
    table = slots + 2 * halo
    here = {"space": lax.axis_index("space"), "batch": lax.axis_index("batch")}
    s = here["space"]
    levels = plan(n_space, n_batch)

    def bit_of(bit):
        return (here[bit[0]] // bit[1]) % 2

    def member(level, flip=0):
        place = 0
        for n, bit in enumerate(levels[level]):
            value = bit_of(bit)
            place = place + (1 - value if flip >> n & 1 else value) * (1 << n)
        return place

    def peer(level, flip):
        there = dict(here)
        for n, bit in enumerate(levels[level]):
            if flip >> n & 1:
                there[bit[0]] = there[bit[0]] + bit[1] * (1 - 2 * bit_of(bit))
        return there

    def flips(level):
        return range(1, 1 << len(levels[level]))

    lower = {**here, "space": s - 1}
    upper = {**here, "space": s + 1}
    has_lower = s > 0
    has_upper = s < n_space - 1

    loads = {}
    pairs = dict(feat=(feat_hbm, feat), send=(send_hbm, send), cot=(cot_hbm, cot), kmap=(kmap_hbm, kmap), w=(w_hbm, w))
    for n, (name, (src, dst)) in enumerate(pairs.items()):
        loads[name] = pltpu.make_async_copy(src, dst, load_sem.at[n])
        loads[name].start()

    lines[...] = lax.broadcasted_iota(jnp.int16, lines.shape, 0)
    barrier = pltpu.get_barrier_semaphore()
    greeted = 0
    for level in range(len(levels)):
        for flip in flips(level):
            pl.semaphore_signal(barrier, inc=1, device_id=peer(level, flip), device_id_type=MESH)
            greeted += 1

    @pl.when(has_lower)
    def _():
        pl.semaphore_signal(barrier, inc=1, device_id=lower, device_id_type=MESH)

    @pl.when(has_upper)
    def _():
        pl.semaphore_signal(barrier, inc=1, device_id=upper, device_id_type=MESH)

    alive = lax.broadcasted_iota(jnp.int32, (slots, channels), 0) < count[0, 0]
    loads["feat"].wait()
    live = jnp.where(alive, feat[...].astype(F32), jnp.zeros((), F32)).astype(BF16)
    ext[:slots] = live
    loads["send"].wait()
    lists = jnp.concatenate([send[0:1, :], send[1:2, :]], 1)
    outgoing[...] = dot(onehot_columns(lists, lines.at[:slots]), live, ((0,), (0,))).astype(BF16)

    @pl.when(s == 0)
    def _():
        ext[slots : slots + halo] = jnp.zeros((halo, channels), BF16)
        back[halo:] = jnp.zeros((halo, channels), F32)

    @pl.when(s == n_space - 1)
    def _():
        ext[slots + halo :] = jnp.zeros((halo, channels), BF16)
        back[:halo] = jnp.zeros((halo, channels), F32)

    neighbours = jnp.minimum(s, 1) + jnp.minimum(n_space - 1 - s, 1)
    pl.semaphore_wait(barrier, greeted + neighbours)

    to_lower = pltpu.make_async_remote_copy(
        src_ref=outgoing.at[:halo], dst_ref=ext.at[pl.ds(slots + halo, halo)],
        send_sem=halo_send.at[0], recv_sem=halo_recv.at[0], device_id=lower, device_id_type=MESH)
    to_upper = pltpu.make_async_remote_copy(
        src_ref=outgoing.at[pl.ds(halo, halo)], dst_ref=ext.at[pl.ds(slots, halo)],
        send_sem=halo_send.at[1], recv_sem=halo_recv.at[1], device_id=upper, device_id_type=MESH)

    def start_both(down, up):
        @pl.when(has_lower)
        def _():
            down.start()

        @pl.when(has_upper)
        def _():
            up.start()

    def wait_both(down, up):
        @pl.when(has_lower)
        def _():
            down.wait_send()
            up.wait_recv()

        @pl.when(has_upper)
        def _():
            up.wait_send()
            down.wait_recv()

    start_both(to_lower, to_upper)

    half, part = TILES // 2, TILES // 8
    half_at = member(0) * half
    part_at = half_at + member(1) * part
    steps = len(levels) + 3
    place = [0] * GROUPS

    def offsets_of(q, flip=0):
        quarter = SIZES[q] // 4
        return pl.ds(FIRSTS[q] + member(2, flip) * quarter, quarter)

    def copies_of(q):
        step = place[q]
        group = pl.ds(FIRSTS[q], SIZES[q])
        quarters = pl.ds(FIRSTS[q] // 4, SIZES[q] // 4)
        level = step if step < len(levels) else steps - 1 - step
        copies = []
        for flip in flips(level):
            if step == 0:
                src = dw.at[group, pl.ds(member(0, flip) * half, half)]
                dst = inbox0.at[group]
            elif step == 1:
                src = dw.at[group, pl.ds(half_at + member(1, flip) * part, part)]
                dst = inbox1.at[flip - 1, group]
            elif step == 2:
                src = dw.at[offsets_of(q, flip), pl.ds(part_at, part)]
                dst = inbox2.at[flip - 1, quarters]
            elif step < len(levels):
                src = dw.at[offsets_of(q), pl.ds(part_at, part)]
                dst = inbox3.at[step - 3, quarters]
            else:
                tiles = pl.ds(half_at, half) if level == 0 else pl.ds(part_at, part)
                src = gw.at[offsets_of(q) if level == 2 else group, tiles]
                dst = src
            sem = (q * steps + step) * 3 + flip - 1
            copies.append(pltpu.make_async_remote_copy(
                src_ref=src, dst_ref=dst, send_sem=sum_send.at[sem], recv_sem=sum_recv.at[sem],
                device_id=peer(level, flip), device_id_type=MESH))
        return copies

    def launch(q):
        for copy in copies_of(q):
            copy.start()

    def advance(q):
        step = place[q]
        if step >= steps:
            return
        for copy in copies_of(q):
            copy.wait()
        group = pl.ds(FIRSTS[q], SIZES[q])
        quarters = pl.ds(FIRSTS[q] // 4, SIZES[q] // 4)
        if step < len(levels):
            if step == 0:
                mine = (group, pl.ds(half_at, half))
                total = dw[mine] + inbox0[group]
            elif step == 1:
                mine = (group, pl.ds(part_at, part))
                total = (dw[mine] + inbox1[0, group]) + (inbox1[1, group] + inbox1[2, group])
            else:
                mine = (offsets_of(q), pl.ds(part_at, part))
                if step == 2:
                    total = (dw[mine] + inbox2[0, quarters]) + (inbox2[1, quarters] + inbox2[2, quarters])
                else:
                    total = dw[mine] + inbox3[step - 3, quarters]
            if step == len(levels) - 1:
                gw[mine] = total * scale
            else:
                dw[mine] = total
        place[q] = step + 1
        if place[q] < steps:
            launch(q)

    def advance_all():
        for q in range(GROUPS):
            advance(q)

    acc[...] = jnp.zeros_like(acc)
    outt[...] = jnp.zeros_like(outt)
    loads["cot"].wait()
    grad[...] = jnp.where(alive, cot[...].astype(F32), jnp.zeros((), F32)).astype(BF16)
    loads["kmap"].wait()
    loads["w"].wait()
    def scatter_step(j, carry):
        weights = w[pl.ds(j * BATCH, BATCH)].reshape(BATCH * channels, channels)
        contrib = dot(grad[...], weights, ((1,), (1,)))
        picks, parts = [], []
        for t in range(BATCH):
            picks.append(onehot_columns(kmap[j * BATCH + t], lines))
            parts.append(split_pair(contrib[:, t * channels : (t + 1) * channels]))
        acc[...] += dot(jnp.concatenate(picks, 1), jnp.concatenate(parts, 0))
        return carry

    scatter_step(0, 0)
    wait_both(to_lower, to_upper)
    extt[...] = ext[...].astype(F32).T.astype(BF16)

    def weight_step(j, carry):
        size = BATCH * channels
        picks = [onehot_columns(kmap[j * BATCH + t], lines) for t in range(BATCH)]
        gathered = jnp.concatenate([dot(extt[...], picked).astype(BF16) for picked in picks], 0)
        gt[pl.ds(pl.multiple_of(j * size, size), size)] = gathered
        products = dot(gathered, grad[...])
        dw[pl.ds(j * BATCH, BATCH)] = products.reshape(BATCH, TILES, ROW, channels)
        return carry

    def forward_step(j, carry):
        weights = w[pl.ds(j * BATCH, BATCH)].reshape(BATCH * channels, channels)
        size = BATCH * channels
        rows = gt[pl.ds(pl.multiple_of(j * size, size), size)]
        outt[...] += dot(weights, rows, ((0,), (0,)))
        return carry

    total_loops = offsets // BATCH
    dw[offsets:] = jnp.zeros((ROUNDED - offsets, TILES, ROW, channels), F32)

    def after_weights(j):
        @pl.when(j == 2)
        def _():
            launch(0)

        @pl.when(j == 3)
        def _():
            advance(0)

        @pl.when(j == 5)
        def _():
            launch(1)

        @pl.when(j == 6)
        def _():
            advance(0)
            advance(1)

        @pl.when(j == 7)
        def _():
            launch(2)

        @pl.when(j == 8)
        def _():
            launch(3)

    def weight_stage(j, carry):
        weight_step(j, carry)
        after_weights(j)
        return carry

    def scatter_stage(ticks, forward):
        def stage(j, carry):
            scatter_step(j, carry)
            if forward:
                forward_step(j, carry)
            for tick in ticks:
                pl.when(j == tick)(lambda tick=tick: advance_all())
            return carry

        return stage

    late = 2 * total_loops // 3
    lax.fori_loop(0, total_loops, weight_stage, 0)
    forward_step(0, 0)
    lax.fori_loop(EARLY, late, scatter_stage((1, 3, 4), True), 0)
    lax.fori_loop(late, total_loops, scatter_stage((6, 8), False), 0)

    both = acc[...]
    gext[...] = both[:, :channels] + both[:, channels:]
    back_lower = pltpu.make_async_remote_copy(
        src_ref=gext.at[pl.ds(slots, halo)], dst_ref=back.at[:halo],
        send_sem=back_send.at[0], recv_sem=back_recv.at[0], device_id=lower, device_id_type=MESH)
    back_upper = pltpu.make_async_remote_copy(
        src_ref=gext.at[pl.ds(slots + halo, halo)], dst_ref=back.at[pl.ds(halo, halo)],
        send_sem=back_send.at[1], recv_sem=back_recv.at[1], device_id=upper, device_id_type=MESH)
    start_both(back_lower, back_upper)

    lax.fori_loop(late, total_loops, forward_step, 0)
    out[...] = jnp.where(alive, outt[...].T, jnp.zeros((), F32)).astype(BF16)

    wait_both(back_lower, back_upper)
    lists = jnp.concatenate([send[1:2, :], send[0:1, :]], 1)
    extra = dot(onehot_columns(lists, lines.at[:slots]), split_pair(back[...]))
    local = gext[:slots] + extra[:, :channels] + extra[:, channels:]
    gfeat[...] = jnp.where(alive, local, jnp.zeros((), F32)).astype(BF16)

    while min(place) < steps:
        advance_all()


def per_device(n_space, n_batch, features, weights, kernel_map, send_rows, counts, cotangent):
    slots, channels = features.shape[1], features.shape[2]
    offsets = weights.shape[0]
    halo = send_rows.shape[2]
    table = slots + 2 * halo
    levels = len(plan(n_space, n_batch))
    steps = levels + 3
    hbm = pl.BlockSpec(memory_space=pltpu.HBM)
    vmem = pl.BlockSpec(memory_space=pltpu.VMEM)
    smem = pl.BlockSpec(memory_space=pltpu.SMEM)
    scale = float((slots * n_space * n_batch) ** -0.5)
    result, grad_features, grad_weights = pl.pallas_call(
        functools.partial(kernel, n_space, n_batch, scale),
        out_shape=(
            jax.ShapeDtypeStruct((slots, channels), BF16),
            jax.ShapeDtypeStruct((slots, channels), BF16),
            jax.ShapeDtypeStruct((ROUNDED, TILES, ROW, channels), F32),
        ),
        in_specs=[hbm, hbm, hbm, hbm, smem, hbm],
        out_specs=(vmem, vmem, vmem),
        scratch_shapes=[
            pltpu.VMEM((slots, channels), BF16),
            pltpu.VMEM((offsets, channels, channels), BF16),
            pltpu.VMEM((offsets, 1, slots), jnp.int32),
            pltpu.VMEM((2, halo), jnp.int32),
            pltpu.VMEM((slots, channels), BF16),
            pltpu.SemaphoreType.DMA((5,)),
            pltpu.VMEM((table, LANES), jnp.int16),
            pltpu.VMEM((table, channels), BF16),
            pltpu.VMEM((2 * halo, channels), BF16),
            pltpu.VMEM((channels, table), BF16),
            pltpu.VMEM((slots, channels), BF16),
            pltpu.VMEM((offsets * channels, slots), BF16),
            pltpu.VMEM((ROUNDED, TILES, ROW, channels), F32),
            pltpu.VMEM((ROUNDED, TILES // 2, ROW, channels), F32),
            pltpu.VMEM((3, ROUNDED, TILES // 8, ROW, channels), F32),
            pltpu.VMEM((3, ROUNDED // 4, TILES // 8, ROW, channels), F32),
            pltpu.VMEM((max(levels - 3, 1), ROUNDED // 4, TILES // 8, ROW, channels), F32),
            pltpu.VMEM((table, 2 * channels), F32),
            pltpu.VMEM((table, channels), F32),
            pltpu.VMEM((2 * halo, channels), F32),
            pltpu.VMEM((channels, slots), F32),
            pltpu.SemaphoreType.DMA((2,)),
            pltpu.SemaphoreType.DMA((2,)),
            pltpu.SemaphoreType.DMA((2,)),
            pltpu.SemaphoreType.DMA((2,)),
            pltpu.SemaphoreType.DMA((GROUPS * steps * 3,)),
            pltpu.SemaphoreType.DMA((GROUPS * steps * 3,)),
        ],
        compiler_params=pltpu.CompilerParams(
            collective_id=0, has_side_effects=True, vmem_limit_bytes=48 * 1024 * 1024
        ),
        name="sparse_conv",
    )(*[pltpu.with_memory_space_constraint(v, pltpu.HBM) for v in (features[0], weights, kernel_map.transpose(1, 0, 2), send_rows[0])], counts, pltpu.with_memory_space_constraint(cotangent[0], pltpu.HBM))
    return (
        result[None],
        grad_features[None],
        grad_weights[:offsets].reshape(offsets, channels, channels),
    )


def solution(mesh):
    in_specs = (
        P("batch", "space", None),
        P(),
        P("batch", None, "space"),
        P("batch", None, "space"),
        P("batch", "space"),
        P("batch", "space", None),
    )
    out_specs = (P("batch", "space", None), P("batch", "space", None), P())
    body = functools.partial(per_device, mesh.shape["space"], mesh.shape["batch"])
    return jax.shard_map(body, mesh=mesh, in_specs=in_specs, out_specs=out_specs, check_vma=False)
```
